512 devices in a mesh: stn: 32 (over z, x_hi), day: 16 (over x_lo, y, core).
Axes of the slice: x: 4 (x_hi: 2, x_lo: 2; x = x_hi * 2 + x_lo), y: 4, z: 16, core: 2. Of those that a mesh axis runs over, the one named last changes fastest.
Arguments:
- records: bfloat16 [1024, 128, 6000], P('stn', 'day'), may hold values from -6 to 6
- offsets: int32 [16], replicated, may hold values from 0 to 15, each once
- pair_order: int32 [1024], replicated, may hold values from 0 to 1023, each once
Outputs:
- stacks: float32 [16, 101, 32768], P(None, None, ('stn', 'day'))
The draws below stay inside these ranges and needn't reach their ends.
Inputs may be any that keep to these rules, and one draw needn't show every extreme that they name: offsets is a permutation of 0 to 15. pair_order is a permutation of 0 to 1023.
All inputs are finite; a program needn't handle non-finite values.
Results may differ from the reference program's by a relative error of at most 0.022.
Values may be sent and summed in bfloat16 or wider, within the bound.
No kernel may reach another device: no remote copies, remote signals or barrier semaphores. Data moves between devices by JAX's collectives and lax.ppermute only.
A program may use at most 64 MiB of HBM per device.

```python
import math
import jax
import jax.numpy as jnp
from jax import lax

SB = 32
DD = 8
NT = 6000
NB = 128
K0 = 30
LAGS = 101
STATIONS = 1024
DAYS = 128
ROUNDS = 16
N_STN = 32
N_DAY = 16


def steps_of(own_key, dims, cuts, smallest, top_value):
    def one(position, blocks):
        steps = jax.random.uniform(jax.random.fold_in(jax.random.fold_in(own_key, 6), position), (blocks,), jnp.float32, smallest / len(cuts), top_value / len(cuts))
        return jnp.repeat(jnp.exp(steps), dims[position] // blocks).reshape((-1,) + (1,) * (len(dims) - position - 1))

    level = one(*cuts[0])
    for cut in cuts[1:]:
        level = level * one(*cut)
    return level


def noise(key, shape, deviation, most, cuts=(), kind=jnp.bfloat16):
    drawn = deviation * jax.random.normal(key, shape, jnp.float32)
    if cuts:
        drawn = drawn * steps_of(key, shape, cuts, -0.22, 0.18)
    return jnp.clip(drawn, -most, most).astype(kind)


def setup_inputs(seed: int = 0) -> dict:
    splits = jax.random.split(jax.random.key(seed), 4)
    return {
        "records": noise(splits[0], (STATIONS, DAYS, NT), 1.0, 6.0, ((0, 32), (1, 16))),
        "offsets": jax.random.permutation(splits[1], ROUNDS).astype(jnp.int32),
        "pair_order": jax.random.permutation(splits[2], SB * SB).astype(jnp.int32),
    }


def phase_rows(column_values):
    band_bins = jnp.arange(NB, dtype=jnp.int32) + K0
    phase_turns = band_bins[:, None] * column_values[None, :] % NT
    phase_angle = 2.0 * math.pi / NT * phase_turns.astype(jnp.float32)
    return jnp.concatenate([jnp.cos(phase_angle), -jnp.sin(phase_angle)], axis=0).astype(jnp.bfloat16)

def spectra_of(block, band_rows):
    station_count = block.shape[0]
    day_count = block.shape[1]
    series = block.astype(jnp.float32).reshape(station_count * day_count, NT)
    series = series - lax.optimization_barrier(jnp.mean(series, axis=1, keepdims=True))
    series = series / jnp.sqrt(lax.optimization_barrier(jnp.mean(series * series, axis=1, keepdims=True)) + 1e-06)
    series = series.astype(jnp.bfloat16)
    raw = lax.dot_general(series, band_rows, (((1,), (1,)), ((), ())), preferred_element_type=jnp.float32)
    raw = raw / jnp.sqrt(lax.optimization_barrier(jnp.sum(raw * raw, axis=1, keepdims=True)) / NB + 1e-06)
    return raw.astype(jnp.bfloat16).reshape(station_count, day_count, 2, NB)

def correlate(own_spectra, partner, lag_rows, weight_scale):
    half_count = own_spectra.shape[1] // 2
    station_count = own_spectra.shape[0]
    turned = jnp.concatenate([own_spectra[:, half_count:], -own_spectra[:, :half_count]], axis=1)
    real_part = jnp.einsum('ick,jck->ijk', own_spectra.astype(jnp.float32), partner.astype(jnp.float32))
    imag_part = jnp.einsum('ick,jck->ijk', turned.astype(jnp.float32), partner.astype(jnp.float32))
    cross_spec = jnp.stack([real_part, imag_part], axis=2).reshape(station_count * station_count, 2 * NB)
    cross_spec = cross_spec.astype(jnp.bfloat16)
    lagged = lax.dot_general(lag_rows, cross_spec, (((0,), (1,)), ((), ())), preferred_element_type=jnp.float32)
    return weight_scale * lagged

def reference(records, offsets, pair_order):
    band_rows = phase_rows(jnp.arange(NT, dtype=jnp.int32))
    lag_rows = phase_rows(jnp.arange(LAGS, dtype=jnp.int32) - LAGS // 2)
    weight_scale = 1.0 / math.sqrt(NB * DAYS)

    def block_spectra(block_index):
        block = lax.dynamic_slice_in_dim(records, (block_index * SB).astype(jnp.int32), SB, 0)
        spectra = spectra_of(block, band_rows).reshape(SB, N_DAY, DD, 2, NB)
        spectra = jnp.transpose(spectra, (1, 0, 3, 2, 4))
        return spectra.reshape(N_DAY, SB, 2 * DD, NB)
    all_spectra = lax.map(block_spectra, jnp.arange(N_STN, dtype=jnp.int32))

    def per_block(block_index):

        def per_round(round_index):
            partner_index = (block_index - offsets[round_index] - 1) % N_STN

            def per_group(group_index):
                own_spectra = all_spectra[block_index, group_index]
                partner = all_spectra[partner_index, group_index]
                lagged = correlate(own_spectra, partner, lag_rows, weight_scale)[:, pair_order]
                rounded = lax.optimization_barrier(lagged.astype(jnp.bfloat16))
                return rounded.astype(jnp.float32)
            return lax.optimization_barrier(jnp.sum(lax.map(per_group, jnp.arange(N_DAY, dtype=jnp.int32)), axis=0))
        return lax.map(per_round, jnp.arange(ROUNDS, dtype=jnp.int32))
    stacked = lax.map(per_block, jnp.arange(N_STN, dtype=jnp.int32))
    return jnp.transpose(stacked, (1, 2, 0, 3)).reshape(ROUNDS, LAGS, N_STN * SB * SB)
```

```python
import functools
import math

import jax
import jax.numpy as jnp
import ml_dtypes
import numpy as np
from jax import lax
from jax.experimental import pallas as pl
from jax.experimental.pallas import tpu as pltpu
from jax.sharding import Mesh
from jax.sharding import PartitionSpec as P

SB = 32
DD = 8
NT = 6000
NB = 128
K0 = 30
LAGS = 101
ROUNDS = 16
N_DAY = 16
N_HI = 2
ZG = 4
NBLK = ZG * N_HI
GROUP = NBLK * N_DAY
BACK = ROUNDS // NBLK
SEEN = ROUNDS + NBLK
KDIM = DD * N_DAY * 2
PAIRS = SB * SB
SHARE = PAIRS // N_DAY
LAG_ROWS = 104
HALF = SB // 2
VMEM = 44 * 1024 * 1024

assert NB == GROUP


def phase_table(columns):
    bins = np.arange(NB, dtype=np.int64) + K0
    turns = (bins[:, None] * columns[None, :]) % NT
    angle = 2.0 * math.pi / NT * turns.astype(np.float64)
    return np.cos(angle).astype(ml_dtypes.bfloat16), (-np.sin(angle)).astype(ml_dtypes.bfloat16)


def band_table():
    real, imag = phase_table(np.arange(NT, dtype=np.int64))
    return np.stack([real, imag], axis=1).reshape(2 * NB, NT)


def lag_table():
    real, imag = phase_table(np.arange(LAGS, dtype=np.int64) - LAGS // 2)
    table = np.zeros((LAG_ROWS, 2 * NB), ml_dtypes.bfloat16)
    table[:LAGS, :NB] = real.T
    table[:LAGS, NB:] = imag.T
    return table


def day_major():
    table = np.zeros((HALF * DD, HALF * DD), ml_dtypes.bfloat16)
    for s in range(HALF):
        for e in range(DD):
            table[s * DD + e, e * HALF + s] = 1
    return table


def spread_rows():
    table = np.zeros((2 * NBLK * SB, NBLK * SB), ml_dtypes.bfloat16)
    for i in range(SB):
        for c in range(2):
            for b in range(NBLK):
                table[i * 2 * NBLK + c * NBLK + b, b * SB + i] = 1
    return table


def pick_rows():
    half = ROUNDS // 2
    table = np.zeros((2 * NBLK * ROUNDS, SEEN * 2 * NBLK), ml_dtypes.bfloat16)
    for h in range(2):
        for b in range(NBLK):
            for s in range(half):
                for c in range(2):
                    met = b + ROUNDS - (h * half + s + 1)
                    row = ((h * NBLK + b) * half + s) * 2 + c
                    table[row, met * 2 * NBLK + c * NBLK + b] = 1
    return table


def spectra_kernel(x_ref, band_ref, order_ref, out_ref):
    x = x_ref[...].astype(jnp.float32).reshape(HALF * DD, NT)
    x = x - jnp.sum(x, axis=1, keepdims=True) * (1.0 / NT)
    power = jnp.sum(x * x, axis=1, keepdims=True) * (1.0 / NT)
    x = (x / jnp.sqrt(power + 1e-06)).astype(jnp.bfloat16)
    raw = lax.dot_general(
        band_ref[...], x, (((1,), (1,)), ((), ())), preferred_element_type=jnp.float32
    )
    scale = jnp.sqrt(jnp.sum(raw * raw, axis=0, keepdims=True) * (1.0 / NB) + 1e-06)
    spectra = (raw / scale).astype(jnp.bfloat16)
    out_ref[...] = jnp.dot(
        spectra, order_ref[...], preferred_element_type=jnp.float32
    ).astype(jnp.bfloat16)


def gather_days_kernel(r_ref, out_ref, wide_ref):
    turned = r_ref[...].astype(jnp.float32).T
    width = 2 * N_DAY
    for half in range(2):
        for e in range(DD):
            row = half * HALF * DD + e * HALF
            for b in range(NBLK):
                wide_ref[b * SB + half * HALF : b * SB + (half + 1) * HALF,
                         e * width : (e + 1) * width] = (
                    turned[row : row + HALF, b * width : (b + 1) * width]
                )
    out_ref[...] = wide_ref[...].astype(jnp.bfloat16)


def cross_kernel(*refs):
    met_refs = refs[: BACK + 1]
    spread_ref, pick_ref, choice_ref, out_ref, cross_ref, pair_ref = refs[BACK + 1 :]
    own = met_refs[0][...]
    wide = own.astype(jnp.float32)
    lane = lax.broadcasted_iota(jnp.int32, wide.shape, 1)
    turned = jnp.where(
        lane % 2 == 0, pltpu.roll(wide, KDIM - 1, 1), -pltpu.roll(wide, 1, 1)
    ).astype(jnp.bfloat16)
    spread = spread_ref[...]
    rows = lax.broadcasted_iota(jnp.int32, (2 * NBLK * SB, KDIM), 0)
    left = jnp.where(
        rows % (2 * NBLK) < NBLK,
        jnp.dot(spread, own, preferred_element_type=jnp.float32),
        jnp.dot(spread, turned, preferred_element_type=jnp.float32),
    ).astype(jnp.bfloat16)
    for step in range(BACK + 1):
        start = (BACK - step) * NBLK * SB
        cross_ref[:, start : start + NBLK * SB] = lax.dot_general(
            left, met_refs[step][...], (((1,), (1,)), ((), ())),
            preferred_element_type=jnp.float32,
        )
    for i in range(SB):
        piece = cross_ref[i * 2 * NBLK : (i + 1) * 2 * NBLK, :]
        for met in range(SEEN):
            pair_ref[met * 2 * NBLK : (met + 1) * 2 * NBLK, i * SB : (i + 1) * SB] = (
                piece[:, met * SB : (met + 1) * SB]
            )
    picked = jnp.dot(
        pick_ref[...], pair_ref[...].astype(jnp.bfloat16), preferred_element_type=jnp.float32
    ).astype(jnp.bfloat16)
    chosen = jnp.dot(picked, choice_ref[...], preferred_element_type=jnp.float32)
    height = ROUNDS
    first = lax.broadcasted_iota(jnp.int32, (height, 2 * SHARE), 1) < SHARE
    for b in range(NBLK):
        for d in range(0, N_DAY, 2):
            low = chosen[b * height : (b + 1) * height, d * SHARE : (d + 2) * SHARE]
            high = chosen[
                (NBLK + b) * height : (NBLK + b + 1) * height, d * SHARE : (d + 2) * SHARE
            ]
            even = jnp.where(first, low, pltpu.roll(high, SHARE, 1))
            odd = jnp.where(first, pltpu.roll(low, SHARE, 1), high)
            out_ref[b * N_DAY + d] = even.astype(jnp.bfloat16)
            out_ref[b * N_DAY + d + 1] = odd.astype(jnp.bfloat16)


def lag_kernel(slot_ref, r_ref, lag_ref, out_ref, wide_ref):
    height = ROUNDS
    half = ROUNDS // 2
    wide_ref[...] = r_ref[...].astype(jnp.float32).reshape(GROUP * height, 2 * SHARE)
    lag = lag_ref[...]
    for s in range(half):
        real = wide_ref[pl.ds(2 * s, GROUP, stride=height), :].astype(jnp.bfloat16)
        imag = wide_ref[pl.ds(2 * s + 1, GROUP, stride=height), :].astype(jnp.bfloat16)
        lagged = jnp.dot(lag[:, :NB], real, preferred_element_type=jnp.float32)
        lagged = lagged + jnp.dot(lag[:, NB:], imag, preferred_element_type=jnp.float32)
        lagged = lagged * (1.0 / math.sqrt(NB * DD * N_DAY))
        out_ref[slot_ref[s]] = lagged[:LAGS, :SHARE]
        out_ref[slot_ref[half + s]] = lagged[:LAGS, SHARE:]


def params():
    return pltpu.CompilerParams(vmem_limit_bytes=VMEM)


def vmem_specs(count):
    return [pl.BlockSpec(memory_space=pltpu.VMEM)] * count


def shards(records, offsets, pair_order):
    group_axes = ("zr", "xh", "day")
    spectra = pl.pallas_call(
        spectra_kernel,
        grid=(2,),
        in_specs=[
            pl.BlockSpec((HALF, DD, NT), lambda i: (i, 0, 0)),
            pl.BlockSpec((2 * NB, NT), lambda i: (0, 0)),
            pl.BlockSpec((HALF * DD, HALF * DD), lambda i: (0, 0)),
        ],
        out_specs=pl.BlockSpec((2 * NB, HALF * DD), lambda i: (0, i)),
        out_shape=jax.ShapeDtypeStruct((2 * NB, SB * DD), jnp.bfloat16),
        compiler_params=params(),
        name="spectra",
    )(records, jnp.asarray(band_table()), jnp.asarray(day_major()))

    by_bin = lax.all_to_all(
        spectra.reshape(GROUP, 2, SB * DD), group_axes, 0, 0, tiled=True
    ).reshape(2 * NB, SB * DD)

    own = pl.pallas_call(
        gather_days_kernel,
        in_specs=vmem_specs(1),
        out_specs=pl.BlockSpec(memory_space=pltpu.VMEM),
        out_shape=jax.ShapeDtypeStruct((NBLK * SB, KDIM), jnp.bfloat16),
        scratch_shapes=[pltpu.VMEM((NBLK * SB, KDIM), jnp.float32)],
        compiler_params=params(),
        name="gather_days",
    )(by_bin)

    groups = lax.axis_size("zq")
    pairs = [(source, (source + 1) % groups) for source in range(groups)]
    met = [own]
    for _ in range(BACK):
        met.append(lax.ppermute(met[-1], "zq", pairs))

    choice = (
        lax.broadcasted_iota(jnp.int32, (PAIRS, PAIRS), 0) == pair_order[None, :]
    ).astype(jnp.bfloat16)

    chosen = pl.pallas_call(
        cross_kernel,
        in_specs=vmem_specs(BACK + 4),
        out_specs=pl.BlockSpec(memory_space=pltpu.VMEM),
        out_shape=jax.ShapeDtypeStruct((GROUP, ROUNDS, 2 * SHARE), jnp.bfloat16),
        scratch_shapes=[
            pltpu.VMEM((2 * NBLK * SB, SEEN * SB), jnp.float32),
            pltpu.VMEM((2 * NBLK * SEEN, PAIRS), jnp.float32),
        ],
        compiler_params=params(),
        name="cross",
    )(*met, jnp.asarray(spread_rows()), jnp.asarray(pick_rows()), choice)

    by_pair = lax.all_to_all(chosen, group_axes, 0, 0, tiled=True)

    steps = jnp.arange(ROUNDS, dtype=jnp.int32)
    slots = jnp.sum(
        jnp.where(offsets[None, :] == steps[:, None], steps[None, :], 0), axis=1
    ).astype(jnp.int32)

    return pl.pallas_call(
        lag_kernel,
        in_specs=[pl.BlockSpec(memory_space=pltpu.SMEM)] + vmem_specs(2),
        out_specs=pl.BlockSpec(memory_space=pltpu.VMEM),
        out_shape=jax.ShapeDtypeStruct((ROUNDS, LAGS, SHARE), jnp.float32),
        scratch_shapes=[pltpu.VMEM((GROUP * ROUNDS, 2 * SHARE), jnp.float32)],
        compiler_params=params(),
        name="lags",
    )(slots, by_pair, jnp.asarray(lag_table()))


def solution(mesh):
    planes = mesh.shape["stn"] // N_HI
    devices = mesh.devices.reshape(planes // ZG, ZG, N_HI, mesh.shape["day"])
    fine = Mesh(devices, ("zq", "zr", "xh", "day"))
    stations = ("zq", "zr", "xh")
    in_specs = (P(stations, "day", None), P(), P())
    out_specs = P(None, None, stations + ("day",))
    return jax.shard_map(
        shards, mesh=fine, in_specs=in_specs, out_specs=out_specs, check_vma=False
    )
```

```python
import functools
import math

import jax
import jax.numpy as jnp
import ml_dtypes
import numpy as np
from jax import lax
from jax.experimental import pallas as pl
from jax.experimental.pallas import tpu as pltpu
from jax.sharding import Mesh
from jax.sharding import PartitionSpec as P

SB = 32
DD = 8
NT = 6000
NB = 128
K0 = 30
LAGS = 101
ROUNDS = 16
N_DAY = 16
N_HI = 2
PLANES = 16
ZG = 1
NBLK = ZG * N_HI
GROUP = NBLK * N_DAY
KB = NB // GROUP
ENT = 2 * KB
MIX = ENT * NBLK
GROUPS = PLANES // ZG
BACK = ROUNDS // NBLK
SEEN = ROUNDS + NBLK
WIDTH = N_DAY * ENT
KDIM = DD * WIDTH
PAIRS = SB * SB
SHARE = PAIRS // N_DAY
LAG_ROWS = 104
HALF = SB // 2
VMEM = 44 * 1024 * 1024

assert NB == GROUP * KB and ROUNDS == BACK * NBLK


def phase_table(columns):
    bins = np.arange(NB, dtype=np.int64) + K0
    turns = (bins[:, None] * columns[None, :]) % NT
    angle = 2.0 * math.pi / NT * turns.astype(np.float64)
    return np.cos(angle).astype(ml_dtypes.bfloat16), (-np.sin(angle)).astype(ml_dtypes.bfloat16)


def band_table():
    real, imag = phase_table(np.arange(NT, dtype=np.int64))
    rows = np.stack([real.reshape(GROUP, KB, NT), imag.reshape(GROUP, KB, NT)], axis=1)
    return rows.reshape(2 * NB, NT)


def lag_table():
    real, imag = phase_table(np.arange(LAGS, dtype=np.int64) - LAGS // 2)
    table = np.zeros((LAG_ROWS, 2 * NB), ml_dtypes.bfloat16)
    rows = np.stack([real.reshape(GROUP, KB, LAGS), imag.reshape(GROUP, KB, LAGS)], axis=0)
    table[:LAGS] = rows.transpose(3, 0, 2, 1).reshape(LAGS, 2 * NB)
    return table


def day_major():
    table = np.zeros((HALF * DD, HALF * DD), ml_dtypes.bfloat16)
    for s in range(HALF):
        for e in range(DD):
            table[s * DD + e, e * HALF + s] = 1
    return table


def spread_rows():
    table = np.zeros((MIX * SB, NBLK * SB), ml_dtypes.bfloat16)
    for i in range(SB):
        for c in range(ENT):
            for b in range(NBLK):
                table[i * MIX + c * NBLK + b, b * SB + i] = 1
    return table


def pick_rows():
    half = ROUNDS // 2
    table = np.zeros((MIX * ROUNDS, SEEN * MIX), ml_dtypes.bfloat16)
    for h in range(2):
        for b in range(NBLK):
            for s in range(half):
                for c in range(ENT):
                    met = b + ROUNDS - (h * half + s + 1)
                    row = ((h * NBLK + b) * half + s) * ENT + c
                    table[row, met * MIX + c * NBLK + b] = 1
    return table


def spectra_kernel(x_ref, band_ref, order_ref, out_ref):
    x = x_ref[...].astype(jnp.float32).reshape(HALF * DD, NT)
    x = x - jnp.sum(x, axis=1, keepdims=True) * (1.0 / NT)
    power = jnp.sum(x * x, axis=1, keepdims=True) * (1.0 / NT)
    x = (x / jnp.sqrt(power + 1e-06)).astype(jnp.bfloat16)
    raw = lax.dot_general(
        band_ref[...], x, (((1,), (1,)), ((), ())), preferred_element_type=jnp.float32
    )
    scale = jnp.sqrt(jnp.sum(raw * raw, axis=0, keepdims=True) * (1.0 / NB) + 1e-06)
    spectra = (raw / scale).astype(jnp.bfloat16)
    out_ref[...] = jnp.dot(
        spectra, order_ref[...], preferred_element_type=jnp.float32
    ).astype(jnp.bfloat16)


def gather_days_kernel(r_ref, out_ref, wide_ref):
    turned = r_ref[...].astype(jnp.float32).T
    for half in range(2):
        for e in range(DD):
            row = half * HALF * DD + e * HALF
            for b in range(NBLK):
                wide_ref[b * SB + half * HALF : b * SB + (half + 1) * HALF,
                         e * WIDTH : (e + 1) * WIDTH] = (
                    turned[row : row + HALF, b * WIDTH : (b + 1) * WIDTH]
                )
    out_ref[...] = wide_ref[...].astype(jnp.bfloat16)


def cross_kernel(
    place_ref, own_ref, all_ref, spread_ref, pick_ref, choice_ref, out_ref, met_ref, cross_ref, pair_ref
):
    own = own_ref[...]
    wide = own.astype(jnp.float32)
    lane = lax.broadcasted_iota(jnp.int32, wide.shape, 1)
    turned = jnp.where(
        lane % ENT < KB, pltpu.roll(wide, KDIM - KB, 1), -pltpu.roll(wide, KB, 1)
    ).astype(jnp.bfloat16)
    spread = spread_ref[...]
    row = lax.broadcasted_iota(jnp.int32, (MIX * SB, KDIM), 0)
    lane = lax.broadcasted_iota(jnp.int32, (MIX * SB, KDIM), 1)
    left = jnp.where(
        row % MIX < MIX // 2,
        jnp.dot(spread, own, preferred_element_type=jnp.float32),
        jnp.dot(spread, turned, preferred_element_type=jnp.float32),
    )
    left = jnp.where(row // NBLK % KB == lane % KB, left, 0.0).astype(jnp.bfloat16)
    height = NBLK * SB
    for step in range(BACK + 1):
        source = lax.rem(place_ref[0] + (GROUPS - BACK + step), GROUPS)
        met_ref[step * height : (step + 1) * height, :] = all_ref[source]
    cross_ref[...] = lax.dot_general(
        left, met_ref[...], (((1,), (1,)), ((), ())), preferred_element_type=jnp.float32
    )
    for i in range(SB):
        piece = cross_ref[i * MIX : (i + 1) * MIX, :]
        for met in range(SEEN):
            pair_ref[met * MIX : (met + 1) * MIX, i * SB : (i + 1) * SB] = (
                piece[:, met * SB : (met + 1) * SB]
            )
    picked = jnp.dot(
        pick_ref[...], pair_ref[...].astype(jnp.bfloat16), preferred_element_type=jnp.float32
    ).astype(jnp.bfloat16)
    chosen = jnp.dot(picked, choice_ref[...], preferred_element_type=jnp.float32)
    height = ROUNDS // 2 * ENT
    first = lax.broadcasted_iota(jnp.int32, (height, 2 * SHARE), 1) < SHARE
    for b in range(NBLK):
        for d in range(0, N_DAY, 2):
            low = chosen[b * height : (b + 1) * height, d * SHARE : (d + 2) * SHARE]
            high = chosen[
                (NBLK + b) * height : (NBLK + b + 1) * height, d * SHARE : (d + 2) * SHARE
            ]
            even = jnp.where(first, low, pltpu.roll(high, SHARE, 1))
            odd = jnp.where(first, pltpu.roll(low, SHARE, 1), high)
            out_ref[b * N_DAY + d] = even.astype(jnp.bfloat16)
            out_ref[b * N_DAY + d + 1] = odd.astype(jnp.bfloat16)


def lag_kernel(slot_ref, r_ref, lag_ref, out_ref, wide_ref):
    half = ROUNDS // 2
    height = half * ENT
    wide_ref[...] = r_ref[...].astype(jnp.float32).reshape(GROUP * height, 2 * SHARE)
    lag = lag_ref[...]
    for s in range(half):
        entries = jnp.concatenate(
            [wide_ref[pl.ds(s * ENT + c, GROUP, stride=height), :] for c in range(ENT)], axis=0
        ).astype(jnp.bfloat16)
        lagged = jnp.dot(lag, entries, preferred_element_type=jnp.float32)
        lagged = lagged * (1.0 / math.sqrt(NB * DD * N_DAY))
        out_ref[slot_ref[s]] = lagged[:LAGS, :SHARE]
        out_ref[slot_ref[half + s]] = lagged[:LAGS, SHARE:]


def params():
    return pltpu.CompilerParams(vmem_limit_bytes=VMEM)


def vmem_specs(count):
    return [pl.BlockSpec(memory_space=pltpu.VMEM)] * count


def shards(records, offsets, pair_order):
    group_axes = ("zr", "xh", "day")
    spectra = pl.pallas_call(
        spectra_kernel,
        grid=(2,),
        in_specs=[
            pl.BlockSpec((HALF, DD, NT), lambda i: (i, 0, 0)),
            pl.BlockSpec((2 * NB, NT), lambda i: (0, 0)),
            pl.BlockSpec((HALF * DD, HALF * DD), lambda i: (0, 0)),
        ],
        out_specs=pl.BlockSpec((2 * NB, HALF * DD), lambda i: (0, i)),
        out_shape=jax.ShapeDtypeStruct((2 * NB, SB * DD), jnp.bfloat16),
        compiler_params=params(),
        name="spectra",
    )(records, jnp.asarray(band_table()), jnp.asarray(day_major()))

    by_bin = lax.all_to_all(
        spectra.reshape(GROUP, ENT, SB * DD), group_axes, 0, 0, tiled=True
    ).reshape(2 * NB, SB * DD)

    own = pl.pallas_call(
        gather_days_kernel,
        in_specs=vmem_specs(1),
        out_specs=pl.BlockSpec(memory_space=pltpu.VMEM),
        out_shape=jax.ShapeDtypeStruct((NBLK * SB, KDIM), jnp.bfloat16),
        scratch_shapes=[pltpu.VMEM((NBLK * SB, KDIM), jnp.float32)],
        compiler_params=params(),
        name="gather_days",
    )(by_bin)

    everyone = lax.all_gather(own, "zq", axis=0)
    place = lax.axis_index("zq").astype(jnp.int32).reshape(1)

    choice = (
        lax.broadcasted_iota(jnp.int32, (PAIRS, PAIRS), 0) == pair_order[None, :]
    ).astype(jnp.bfloat16)

    chosen = pl.pallas_call(
        cross_kernel,
        in_specs=[pl.BlockSpec(memory_space=pltpu.SMEM)] + vmem_specs(5),
        out_specs=pl.BlockSpec(memory_space=pltpu.VMEM),
        out_shape=jax.ShapeDtypeStruct((GROUP, ROUNDS // 2 * ENT, 2 * SHARE), jnp.bfloat16),
        scratch_shapes=[
            pltpu.VMEM((SEEN * SB, KDIM), jnp.bfloat16),
            pltpu.VMEM((MIX * SB, SEEN * SB), jnp.float32),
            pltpu.VMEM((MIX * SEEN, PAIRS), jnp.float32),
        ],
        compiler_params=params(),
        name="cross",
    )(place, own, everyone, jnp.asarray(spread_rows()), jnp.asarray(pick_rows()), choice)

    by_pair = lax.all_to_all(chosen, group_axes, 0, 0, tiled=True)

    steps = jnp.arange(ROUNDS, dtype=jnp.int32)
    slots = jnp.sum(
        jnp.where(offsets[None, :] == steps[:, None], steps[None, :], 0), axis=1
    ).astype(jnp.int32)

    return pl.pallas_call(
        lag_kernel,
        in_specs=[pl.BlockSpec(memory_space=pltpu.SMEM)] + vmem_specs(2),
        out_specs=pl.BlockSpec(memory_space=pltpu.VMEM),
        out_shape=jax.ShapeDtypeStruct((ROUNDS, LAGS, SHARE), jnp.float32),
        scratch_shapes=[pltpu.VMEM((GROUP * ROUNDS // 2 * ENT, 2 * SHARE), jnp.float32)],
        compiler_params=params(),
        name="lags",
    )(slots, by_pair, jnp.asarray(lag_table()))


def solution(mesh):
    planes = mesh.shape["stn"] // N_HI
    devices = mesh.devices.reshape(planes // ZG, ZG, N_HI, mesh.shape["day"])
    fine = Mesh(devices, ("zq", "zr", "xh", "day"))
    stations = ("zq", "zr", "xh")
    in_specs = (P(stations, "day", None), P(), P())
    out_specs = P(None, None, stations + ("day",))
    return jax.shard_map(
        shards, mesh=fine, in_specs=in_specs, out_specs=out_specs, check_vma=False
    )
```

```python
import functools
import math

import jax
import jax.numpy as jnp
import ml_dtypes
import numpy as np
from jax import lax
from jax.experimental import pallas as pl
from jax.experimental.pallas import tpu as pltpu
from jax.sharding import Mesh
from jax.sharding import PartitionSpec as P

SB = 32
DD = 8
NT = 6000
NB = 128
K0 = 30
LAGS = 101
ROUNDS = 16
N_DAY = 16
N_HI = 2
PLANES = 16
ZG = 2
NBLK = ZG * N_HI
GROUP = NBLK * N_DAY
KB = NB // GROUP
ENT = 2 * KB
MIX = ENT * NBLK
GROUPS = PLANES // ZG
BACK = ROUNDS // NBLK
SEEN = ROUNDS + NBLK
WIDTH = N_DAY * ENT
KDIM = DD * WIDTH
PAIRS = SB * SB
SHARE = PAIRS // N_DAY
LAG_ROWS = 104
HALF = SB // 2
STREAMS = 2
VMEM = 44 * 1024 * 1024

assert NB == GROUP * KB and ROUNDS == BACK * NBLK


def phase_table(columns):
    bins = np.arange(NB, dtype=np.int64) + K0
    turns = (bins[:, None] * columns[None, :]) % NT
    angle = 2.0 * math.pi / NT * turns.astype(np.float64)
    return np.cos(angle).astype(ml_dtypes.bfloat16), (-np.sin(angle)).astype(ml_dtypes.bfloat16)


def band_table():
    real, imag = phase_table(np.arange(NT, dtype=np.int64))
    rows = np.stack([real.reshape(GROUP, KB, NT), imag.reshape(GROUP, KB, NT)], axis=1)
    return rows.reshape(2 * NB, NT)


def lag_table():
    real, imag = phase_table(np.arange(LAGS, dtype=np.int64) - LAGS // 2)
    table = np.zeros((LAG_ROWS, 2 * NB), ml_dtypes.bfloat16)
    rows = np.stack([real.reshape(GROUP, KB, LAGS), imag.reshape(GROUP, KB, LAGS)], axis=0)
    table[:LAGS] = rows.transpose(3, 0, 2, 1).reshape(LAGS, 2 * NB)
    return table


def day_major():
    table = np.zeros((HALF * DD, HALF * DD), ml_dtypes.bfloat16)
    for s in range(HALF):
        for e in range(DD):
            table[s * DD + e, e * HALF + s] = 1
    return table


def spread_rows():
    table = np.zeros((MIX * SB, NBLK * SB), ml_dtypes.bfloat16)
    for i in range(SB):
        for c in range(ENT):
            for b in range(NBLK):
                table[i * MIX + c * NBLK + b, b * SB + i] = 1
    return table


def pick_rows():
    half = ROUNDS // 2
    table = np.zeros((MIX * ROUNDS, SEEN * MIX), ml_dtypes.bfloat16)
    for h in range(2):
        for b in range(NBLK):
            for s in range(half):
                for c in range(ENT):
                    met = b + ROUNDS - (h * half + s + 1)
                    row = ((h * NBLK + b) * half + s) * ENT + c
                    table[row, met * MIX + c * NBLK + b] = 1
    return table


def spectra_kernel(x_ref, band_ref, order_ref, out_ref):
    x = x_ref[...].astype(jnp.float32).reshape(HALF * DD, NT)
    x = x - jnp.sum(x, axis=1, keepdims=True) * (1.0 / NT)
    power = jnp.sum(x * x, axis=1, keepdims=True) * (1.0 / NT)
    x = (x / jnp.sqrt(power + 1e-06)).astype(jnp.bfloat16)
    raw = lax.dot_general(
        band_ref[...], x, (((1,), (1,)), ((), ())), preferred_element_type=jnp.float32
    )
    scale = jnp.sqrt(jnp.sum(raw * raw, axis=0, keepdims=True) * (1.0 / NB) + 1e-06)
    spectra = (raw / scale).astype(jnp.bfloat16)
    out_ref[...] = jnp.dot(
        spectra, order_ref[...], preferred_element_type=jnp.float32
    ).astype(jnp.bfloat16)


def gather_days_kernel(r_ref, *refs):
    out_refs, wide_ref = refs[:-1], refs[-1]
    turned = r_ref[...].astype(jnp.float32).T
    for half in range(2):
        for e in range(DD):
            row = half * HALF * DD + e * HALF
            for b in range(NBLK):
                wide_ref[b * SB + half * HALF : b * SB + (half + 1) * HALF,
                         e * WIDTH : (e + 1) * WIDTH] = (
                    turned[row : row + HALF, b * WIDTH : (b + 1) * WIDTH]
                )
    share = NBLK * SB // STREAMS
    for part, out_ref in enumerate(out_refs):
        out_ref[...] = wide_ref[part * share : (part + 1) * share, :].astype(jnp.bfloat16)


def cross_kernel(*refs):
    piece_refs = refs[: (BACK + 1) * STREAMS]
    spread_ref, pick_ref, choice_ref, out_ref, met_ref, cross_ref, pair_ref = refs[
        (BACK + 1) * STREAMS :
    ]
    share = NBLK * SB // STREAMS
    for step in range(BACK + 1):
        for part in range(STREAMS):
            start = (BACK - step) * NBLK * SB + part * share
            met_ref[start : start + share, :] = piece_refs[step * STREAMS + part][...]
    own = met_ref[BACK * NBLK * SB :, :]
    wide = own.astype(jnp.float32)
    lane = lax.broadcasted_iota(jnp.int32, wide.shape, 1)
    turned = jnp.where(
        lane % ENT < KB, pltpu.roll(wide, KDIM - KB, 1), -pltpu.roll(wide, KB, 1)
    ).astype(jnp.bfloat16)
    spread = spread_ref[...]
    row = lax.broadcasted_iota(jnp.int32, (MIX * SB, KDIM), 0)
    lane = lax.broadcasted_iota(jnp.int32, (MIX * SB, KDIM), 1)
    left = jnp.where(
        row % MIX < MIX // 2,
        jnp.dot(spread, own, preferred_element_type=jnp.float32),
        jnp.dot(spread, turned, preferred_element_type=jnp.float32),
    )
    left = jnp.where(row // NBLK % KB == lane % KB, left, 0.0).astype(jnp.bfloat16)
    cross_ref[...] = lax.dot_general(
        left, met_ref[...], (((1,), (1,)), ((), ())), preferred_element_type=jnp.float32
    )
    for i in range(SB):
        piece = cross_ref[i * MIX : (i + 1) * MIX, :]
        for met in range(SEEN):
            pair_ref[met * MIX : (met + 1) * MIX, i * SB : (i + 1) * SB] = (
                piece[:, met * SB : (met + 1) * SB]
            )
    picked = jnp.dot(
        pick_ref[...], pair_ref[...].astype(jnp.bfloat16), preferred_element_type=jnp.float32
    ).astype(jnp.bfloat16)
    chosen = jnp.dot(picked, choice_ref[...], preferred_element_type=jnp.float32)
    height = ROUNDS // 2 * ENT
    first = lax.broadcasted_iota(jnp.int32, (height, 2 * SHARE), 1) < SHARE
    for b in range(NBLK):
        for d in range(0, N_DAY, 2):
            low = chosen[b * height : (b + 1) * height, d * SHARE : (d + 2) * SHARE]
            high = chosen[
                (NBLK + b) * height : (NBLK + b + 1) * height, d * SHARE : (d + 2) * SHARE
            ]
            even = jnp.where(first, low, pltpu.roll(high, SHARE, 1))
            odd = jnp.where(first, pltpu.roll(low, SHARE, 1), high)
            out_ref[b * N_DAY + d] = even.astype(jnp.bfloat16)
            out_ref[b * N_DAY + d + 1] = odd.astype(jnp.bfloat16)


def lag_kernel(slot_ref, r_ref, lag_ref, out_ref, wide_ref):
    half = ROUNDS // 2
    height = half * ENT
    wide_ref[...] = r_ref[...].astype(jnp.float32).reshape(GROUP * height, 2 * SHARE)
    lag = lag_ref[...]
    for s in range(half):
        entries = jnp.concatenate(
            [wide_ref[pl.ds(s * ENT + c, GROUP, stride=height), :] for c in range(ENT)], axis=0
        ).astype(jnp.bfloat16)
        lagged = lax.dot_general(
            entries, lag, (((0,), (1,)), ((), ())), preferred_element_type=jnp.float32
        )
        lagged = lagged * (1.0 / math.sqrt(NB * DD * N_DAY))
        out_ref[slot_ref[s]] = lagged[:SHARE, :LAGS]
        out_ref[slot_ref[half + s]] = lagged[SHARE:, :LAGS]


def params():
    return pltpu.CompilerParams(vmem_limit_bytes=VMEM)


def vmem_specs(count):
    return [pl.BlockSpec(memory_space=pltpu.VMEM)] * count


def shards(records, offsets, pair_order):
    group_axes = ("zr", "xh", "day")
    spectra = pl.pallas_call(
        spectra_kernel,
        grid=(2,),
        in_specs=[
            pl.BlockSpec((HALF, DD, NT), lambda i: (i, 0, 0)),
            pl.BlockSpec((2 * NB, NT), lambda i: (0, 0)),
            pl.BlockSpec((HALF * DD, HALF * DD), lambda i: (0, 0)),
        ],
        out_specs=pl.BlockSpec((2 * NB, HALF * DD), lambda i: (0, i)),
        out_shape=jax.ShapeDtypeStruct((2 * NB, SB * DD), jnp.bfloat16),
        compiler_params=params(),
        name="spectra",
    )(records, jnp.asarray(band_table()), jnp.asarray(day_major()))

    by_bin = lax.all_to_all(
        spectra.reshape(GROUP, ENT, SB * DD), group_axes, 0, 0, tiled=True
    ).reshape(2 * NB, SB * DD)

    own = pl.pallas_call(
        gather_days_kernel,
        in_specs=vmem_specs(1),
        out_specs=vmem_specs(STREAMS),
        out_shape=[jax.ShapeDtypeStruct((NBLK * SB // STREAMS, KDIM), jnp.bfloat16)] * STREAMS,
        scratch_shapes=[pltpu.VMEM((NBLK * SB, KDIM), jnp.float32)],
        compiler_params=params(),
        name="gather_days",
    )(by_bin)

    pairs = [(source, (source + 1) % GROUPS) for source in range(GROUPS)]
    pieces = list(own)
    for step in range(BACK):
        pieces += [lax.ppermute(piece, "zq", pairs) for piece in pieces[step * STREAMS :]]

    choice = (
        lax.broadcasted_iota(jnp.int32, (PAIRS, PAIRS), 0) == pair_order[None, :]
    ).astype(jnp.bfloat16)

    chosen = pl.pallas_call(
        cross_kernel,
        in_specs=vmem_specs((BACK + 1) * STREAMS + 3),
        out_specs=pl.BlockSpec(memory_space=pltpu.VMEM),
        out_shape=jax.ShapeDtypeStruct((GROUP, ROUNDS // 2 * ENT, 2 * SHARE), jnp.bfloat16),
        scratch_shapes=[
            pltpu.VMEM((SEEN * SB, KDIM), jnp.bfloat16),
            pltpu.VMEM((MIX * SB, SEEN * SB), jnp.float32),
            pltpu.VMEM((MIX * SEEN, PAIRS), jnp.float32),
        ],
        compiler_params=params(),
        name="cross",
    )(*pieces, jnp.asarray(spread_rows()), jnp.asarray(pick_rows()), choice)

    by_pair = lax.all_to_all(chosen, group_axes, 0, 0, tiled=True)

    steps = jnp.arange(ROUNDS, dtype=jnp.int32)
    slots = jnp.sum(
        jnp.where(offsets[None, :] == steps[:, None], steps[None, :], 0), axis=1
    ).astype(jnp.int32)

    lagged = pl.pallas_call(
        lag_kernel,
        in_specs=[pl.BlockSpec(memory_space=pltpu.SMEM)] + vmem_specs(2),
        out_specs=pl.BlockSpec(memory_space=pltpu.VMEM),
        out_shape=jax.ShapeDtypeStruct((ROUNDS, SHARE, LAGS), jnp.float32),
        scratch_shapes=[pltpu.VMEM((GROUP * ROUNDS // 2 * ENT, 2 * SHARE), jnp.float32)],
        compiler_params=params(),
        name="lags",
    )(slots, by_pair, jnp.asarray(lag_table()))
    return jnp.transpose(lagged, (0, 2, 1))


def solution(mesh):
    planes = mesh.shape["stn"] // N_HI
    devices = mesh.devices.reshape(planes // ZG, ZG, N_HI, mesh.shape["day"])
    fine = Mesh(devices, ("zq", "zr", "xh", "day"))
    stations = ("zq", "zr", "xh")
    in_specs = (P(stations, "day", None), P(), P())
    out_specs = P(None, None, stations + ("day",))
    return jax.shard_map(
        shards, mesh=fine, in_specs=in_specs, out_specs=out_specs, check_vma=False
    )
```

```python
import functools
import math

import jax
import jax.numpy as jnp
import ml_dtypes
import numpy as np
from jax import lax
from jax.experimental import pallas as pl
from jax.experimental.pallas import tpu as pltpu
from jax.sharding import Mesh
from jax.sharding import PartitionSpec as P

SB = 32
DD = 8
NT = 6000
NB = 128
K0 = 30
LAGS = 101
ROUNDS = 16
N_DAY = 16
N_HI = 2
PLANES = 16
ZG = 2
NBLK = ZG * N_HI
GROUP = NBLK * N_DAY
KB = NB // GROUP
ENT = 2 * KB
MIX = ENT * NBLK
GROUPS = PLANES // ZG
BACK = ROUNDS // NBLK
SEEN = ROUNDS + NBLK
WIDTH = N_DAY * ENT
KDIM = DD * WIDTH
PAIRS = SB * SB
SHARE = PAIRS // N_DAY
LAG_ROWS = 128
STEPS = 16 // ENT
BASE = 256
FETCHES = 8
VMEM = 44 * 1024 * 1024

assert NB == GROUP * KB and ROUNDS == BACK * NBLK


def phase_table(columns):
    bins = np.arange(NB, dtype=np.int64) + K0
    turns = (bins[:, None] * columns[None, :]) % NT
    angle = 2.0 * math.pi / NT * turns.astype(np.float64)
    return np.cos(angle).astype(ml_dtypes.bfloat16), (-np.sin(angle)).astype(ml_dtypes.bfloat16)


def band_parts():
    bins = (np.arange(NB) + K0).reshape(GROUP, 1, KB)
    bins = np.broadcast_to(bins, (GROUP, 2, KB)).reshape(2 * NB).astype(np.int64)
    imag = np.broadcast_to(np.arange(2).reshape(1, 2, 1), (GROUP, 2, KB)).reshape(2 * NB)
    unit = 2.0 * math.pi / NT
    fine = unit * (np.arange(BASE)[:, None] * bins % NT)
    coarse = unit * (np.arange(0, NT, BASE)[:, None] * bins % NT)
    with_cos = np.where(imag, -np.sin(coarse), np.cos(coarse))
    with_sin = np.where(imag, -np.cos(coarse), -np.sin(coarse))
    parts = np.concatenate([np.cos(fine), np.sin(fine), with_cos, with_sin], axis=0)
    return np.pad(parts, ((0, -len(parts) % 8), (0, 0))).astype(np.float32)


def lag_table():
    real, imag = phase_table(np.arange(LAGS, dtype=np.int64) - LAGS // 2)
    rows = np.stack([real.reshape(GROUP, KB, LAGS), imag.reshape(GROUP, KB, LAGS)], axis=1)
    rows = rows.reshape(GROUP, ENT, LAGS).transpose(2, 0, 1)
    table = np.zeros((STEPS, LAG_ROWS, GROUP, STEPS, ENT), ml_dtypes.bfloat16)
    for step in range(STEPS):
        table[step, :LAGS, :, step, :] = rows
    return table.reshape(STEPS * LAG_ROWS, GROUP * STEPS * ENT)


def spread_rows():
    table = np.zeros((MIX * SB, NBLK * SB), ml_dtypes.bfloat16)
    for i in range(SB):
        for c in range(ENT):
            for b in range(NBLK):
                table[i * MIX + c * NBLK + b, b * SB + i] = 1
    return table


def pick_rows():
    half = ROUNDS // 2
    table = np.zeros((MIX * ROUNDS, SEEN * MIX), ml_dtypes.bfloat16)
    for h in range(2):
        for b in range(NBLK):
            for s in range(half):
                for c in range(ENT):
                    met = b + ROUNDS - (h * half + s + 1)
                    row = ((h * NBLK + b) * half + s) * ENT + c
                    table[row, met * MIX + c * NBLK + b] = 1
    return table


def spectra_kernel(records_ref, parts_ref, out_ref, x_ref, angle_ref, centred_ref, sems):
    part = SB // FETCHES
    copies = [
        pltpu.make_async_copy(
            records_ref.at[pl.ds(i * part, part)], x_ref.at[pl.ds(i * part, part)], sems.at[i]
        )
        for i in range(FETCHES)
    ]
    angles = pltpu.make_async_copy(parts_ref, angle_ref, sems.at[FETCHES])
    angles.start()
    for copy in copies:
        copy.start()
    powers = []
    for i, copy in enumerate(copies):
        copy.wait()
        x = x_ref[i * part : (i + 1) * part].astype(jnp.float32).reshape(part * DD, NT)
        x = x - jnp.sum(x, axis=1, keepdims=True) * (1.0 / NT)
        powers.append(jnp.sum(x * x, axis=1, keepdims=True) * (1.0 / NT))
        centred_ref[i * part * DD : (i + 1) * part * DD, :] = x.astype(jnp.bfloat16)
    power = jnp.concatenate(powers, axis=0)
    angles.wait()
    blocks = pl.cdiv(NT, BASE)
    raw = jnp.zeros((SB * DD, 2 * NB), jnp.float32)
    for block in range(blocks):
        start, size = block * BASE, min(BASE, NT - block * BASE)
        with_cos = angle_ref[2 * BASE + block : 2 * BASE + block + 1, :]
        with_sin = angle_ref[2 * BASE + blocks + block : 2 * BASE + blocks + block + 1, :]
        table = with_cos * angle_ref[:size, :] + with_sin * angle_ref[BASE : BASE + size, :]
        raw = raw + jnp.dot(
            centred_ref[:, start : start + size], table.astype(jnp.bfloat16),
            preferred_element_type=jnp.float32,
        )
    raw = raw / jnp.sqrt(power + 1e-06)
    scale = jnp.sqrt(jnp.sum(raw * raw, axis=1, keepdims=True) * (1.0 / NB) + 1e-06)
    spectra = (raw / scale).astype(jnp.bfloat16)
    row = lax.broadcasted_iota(jnp.int32, (SB * DD, SB * DD), 0)
    column = lax.broadcasted_iota(jnp.int32, (SB * DD, SB * DD), 1)
    order = (row == column % SB * DD + column // SB).astype(jnp.float32).astype(jnp.bfloat16)
    by_entry = lax.dot_general(
        spectra, order, (((0,), (0,)), ((), ())), preferred_element_type=jnp.float32
    )
    for device in range(GROUP):
        out_ref[device] = by_entry[device * ENT : (device + 1) * ENT, :].astype(jnp.bfloat16)


def gather_days_kernel(r_ref, out_ref, wide_ref):
    turned = r_ref[...].astype(jnp.float32).T
    for e in range(DD):
        for b in range(NBLK):
            wide_ref[b * SB : (b + 1) * SB, e * WIDTH : (e + 1) * WIDTH] = (
                turned[e * SB : (e + 1) * SB, b * WIDTH : (b + 1) * WIDTH]
            )
    out_ref[...] = wide_ref[...].astype(jnp.bfloat16)


def cross_kernel(*refs):
    group_refs = refs[: BACK + 1]
    spread_ref, pick_ref, choice_ref, out_ref, met_ref, cross_ref, pair_ref = refs[BACK + 1 :]
    for step, group_ref in enumerate(group_refs):
        start = (BACK - step) * NBLK * SB
        met_ref[start : start + NBLK * SB, :] = group_ref[...]
    own = met_ref[BACK * NBLK * SB :, :]
    wide = own.astype(jnp.float32)
    lane = lax.broadcasted_iota(jnp.int32, wide.shape, 1)
    turned = jnp.where(
        lane % ENT < KB, pltpu.roll(wide, KDIM - KB, 1), -pltpu.roll(wide, KB, 1)
    ).astype(jnp.bfloat16)
    spread = spread_ref[...]
    row = lax.broadcasted_iota(jnp.int32, (MIX * SB, KDIM), 0)
    lane = lax.broadcasted_iota(jnp.int32, (MIX * SB, KDIM), 1)
    left = jnp.where(
        row % MIX < MIX // 2,
        jnp.dot(spread, own, preferred_element_type=jnp.float32),
        jnp.dot(spread, turned, preferred_element_type=jnp.float32),
    )
    left = jnp.where(row // NBLK % KB == lane % KB, left, 0.0).astype(jnp.bfloat16)
    cross_ref[...] = lax.dot_general(
        left, met_ref[...], (((1,), (1,)), ((), ())), preferred_element_type=jnp.float32
    )
    for i in range(SB):
        piece = cross_ref[i * MIX : (i + 1) * MIX, :]
        for met in range(SEEN):
            pair_ref[met * MIX : (met + 1) * MIX, i * SB : (i + 1) * SB] = (
                piece[:, met * SB : (met + 1) * SB]
            )
    picked = jnp.dot(
        pick_ref[...], pair_ref[...].astype(jnp.bfloat16), preferred_element_type=jnp.float32
    ).astype(jnp.bfloat16)
    chosen = jnp.dot(picked, choice_ref[...], preferred_element_type=jnp.float32)
    height = ROUNDS // 2 * ENT
    first = lax.broadcasted_iota(jnp.int32, (height, 2 * SHARE), 1) < SHARE
    for b in range(NBLK):
        for d in range(0, N_DAY, 2):
            low = chosen[b * height : (b + 1) * height, d * SHARE : (d + 2) * SHARE]
            high = chosen[
                (NBLK + b) * height : (NBLK + b + 1) * height, d * SHARE : (d + 2) * SHARE
            ]
            even = jnp.where(first, low, pltpu.roll(high, SHARE, 1))
            odd = jnp.where(first, pltpu.roll(low, SHARE, 1), high)
            out_ref[b * N_DAY + d] = even.astype(jnp.bfloat16)
            out_ref[b * N_DAY + d + 1] = odd.astype(jnp.bfloat16)


def lag_kernel(slot_ref, r_ref, lag_ref, out_ref):
    half = ROUNDS // 2
    lag = lag_ref[...]
    for first in range(0, half, STEPS):
        entries = r_ref[:, first * ENT : (first + STEPS) * ENT, :].reshape(
            GROUP * STEPS * ENT, 2 * SHARE
        )
        lagged = jnp.dot(lag, entries, preferred_element_type=jnp.float32)
        lagged = lagged * (1.0 / math.sqrt(NB * DD * N_DAY))
        for step in range(STEPS):
            turned = lagged[step * LAG_ROWS : (step + 1) * LAG_ROWS, :].T
            out_ref[slot_ref[first + step]] = turned[:SHARE, :LAGS]
            out_ref[slot_ref[half + first + step]] = turned[SHARE:, :LAGS]


def params():
    return pltpu.CompilerParams(vmem_limit_bytes=VMEM)


def vmem_specs(count):
    return [pl.BlockSpec(memory_space=pltpu.VMEM)] * count


def shards(records, offsets, pair_order):
    group_axes = ("zr", "xh", "day")
    parts = band_parts()
    spectra = pl.pallas_call(
        spectra_kernel,
        in_specs=[pl.BlockSpec(memory_space=pltpu.HBM)] * 2,
        out_specs=pl.BlockSpec(memory_space=pltpu.VMEM),
        out_shape=jax.ShapeDtypeStruct((GROUP, ENT, SB * DD), jnp.bfloat16),
        scratch_shapes=[
            pltpu.VMEM((SB, DD, NT), jnp.bfloat16),
            pltpu.VMEM(parts.shape, jnp.float32),
            pltpu.VMEM((SB * DD, NT), jnp.bfloat16),
            pltpu.SemaphoreType.DMA((FETCHES + 1,)),
        ],
        compiler_params=pltpu.CompilerParams(vmem_limit_bytes=62 * 1024 * 1024),
        name="spectra",
    )(records, jnp.asarray(parts))

    by_bin = lax.all_to_all(spectra, group_axes, 0, 0, tiled=True).reshape(2 * NB, SB * DD)

    own = pl.pallas_call(
        gather_days_kernel,
        in_specs=vmem_specs(1),
        out_specs=pl.BlockSpec(memory_space=pltpu.VMEM),
        out_shape=jax.ShapeDtypeStruct((NBLK * SB, KDIM), jnp.bfloat16),
        scratch_shapes=[pltpu.VMEM((NBLK * SB, KDIM), jnp.float32)],
        compiler_params=params(),
        name="gather_days",
    )(by_bin)

    def moved(piece, steps):
        pairs = [(source, (source + steps) % GROUPS) for source in range(GROUPS)]
        return lax.ppermute(piece, "zq", pairs)

    met, far = [own], own
    for _ in range(BACK - 1):
        met.append(moved(met[-1], 1))
    for _ in range(2):
        far = moved(far, -(GROUPS - BACK) // 2)
    met.append(far)

    choice = (
        lax.broadcasted_iota(jnp.int32, (PAIRS, PAIRS), 0) == pair_order[None, :]
    ).astype(jnp.bfloat16)

    chosen = pl.pallas_call(
        cross_kernel,
        in_specs=vmem_specs(BACK + 4),
        out_specs=pl.BlockSpec(memory_space=pltpu.VMEM),
        out_shape=jax.ShapeDtypeStruct((GROUP, ROUNDS // 2 * ENT, 2 * SHARE), jnp.bfloat16),
        scratch_shapes=[
            pltpu.VMEM((SEEN * SB, KDIM), jnp.bfloat16),
            pltpu.VMEM((MIX * SB, SEEN * SB), jnp.float32),
            pltpu.VMEM((MIX * SEEN, PAIRS), jnp.float32),
        ],
        compiler_params=params(),
        name="cross",
    )(*met, jnp.asarray(spread_rows()), jnp.asarray(pick_rows()), choice)

    by_pair = lax.all_to_all(chosen, group_axes, 0, 0, tiled=True)

    steps = jnp.arange(ROUNDS, dtype=jnp.int32)
    slots = jnp.sum(
        jnp.where(offsets[None, :] == steps[:, None], steps[None, :], 0), axis=1
    ).astype(jnp.int32)

    lagged = pl.pallas_call(
        lag_kernel,
        in_specs=[pl.BlockSpec(memory_space=pltpu.SMEM)] + vmem_specs(2),
        out_specs=pl.BlockSpec(memory_space=pltpu.VMEM),
        out_shape=jax.ShapeDtypeStruct((ROUNDS, SHARE, LAGS), jnp.float32),
        compiler_params=params(),
        name="lags",
    )(slots, by_pair, jnp.asarray(lag_table()))
    return jnp.transpose(lagged, (0, 2, 1))


def solution(mesh):
    planes = mesh.shape["stn"] // N_HI
    devices = mesh.devices.reshape(planes // ZG, ZG, N_HI, mesh.shape["day"])
    fine = Mesh(devices, ("zq", "zr", "xh", "day"))
    stations = ("zq", "zr", "xh")
    in_specs = (P(stations, "day", None), P(), P())
    out_specs = P(None, None, stations + ("day",))
    return jax.shard_map(
        shards, mesh=fine, in_specs=in_specs, out_specs=out_specs, check_vma=False
    )
```

```python
import functools
import math

import jax
import jax.numpy as jnp
import ml_dtypes
import numpy as np
from jax import lax
from jax.experimental import pallas as pl
from jax.experimental.pallas import tpu as pltpu
from jax.sharding import Mesh
from jax.sharding import PartitionSpec as P

SB = 32
DD = 8
NT = 6000
NB = 128
K0 = 30
LAGS = 101
ROUNDS = 16
N_DAY = 16
N_HI = 2
PLANES = 16
ZG = 2
NBLK = ZG * N_HI
GROUP = NBLK * N_DAY
KB = NB // GROUP
ENT = 2 * KB
MIX = ENT * NBLK
GROUPS = PLANES // ZG
BACK = ROUNDS // NBLK
SEEN = ROUNDS + NBLK
WIDTH = N_DAY * ENT
KDIM = DD * WIDTH
PAIRS = SB * SB
SHARE = PAIRS // N_DAY
LAG_ROWS = 128
STEPS = 16 // ENT
BASE = 256
PIECE = 1536
PIECES = [(start, min(PIECE, NT - start)) for start in range(0, NT, PIECE)]
VMEM = 44 * 1024 * 1024

assert NB == GROUP * KB and ROUNDS == BACK * NBLK


def phase_table(columns):
    bins = np.arange(NB, dtype=np.int64) + K0
    turns = (bins[:, None] * columns[None, :]) % NT
    angle = 2.0 * math.pi / NT * turns.astype(np.float64)
    return np.cos(angle).astype(ml_dtypes.bfloat16), (-np.sin(angle)).astype(ml_dtypes.bfloat16)


def band_parts():
    bins = (np.arange(NB) + K0).reshape(GROUP, 1, KB)
    bins = np.broadcast_to(bins, (GROUP, 2, KB)).reshape(2 * NB).astype(np.int64)
    imag = np.broadcast_to(np.arange(2).reshape(1, 2, 1), (GROUP, 2, KB)).reshape(2 * NB)
    unit = 2.0 * math.pi / NT
    fine = unit * (np.arange(BASE)[:, None] * bins % NT)
    coarse = unit * (np.arange(0, NT, BASE)[:, None] * bins % NT)
    with_cos = np.where(imag, -np.sin(coarse), np.cos(coarse))
    with_sin = np.where(imag, -np.cos(coarse), -np.sin(coarse))
    real, imag = phase_table(np.arange(NT, dtype=np.int64))
    sums = np.stack([real.reshape(GROUP, KB, NT), imag.reshape(GROUP, KB, NT)], axis=1)
    sums = sums.astype(np.float64).sum(axis=3).reshape(1, 2 * NB)
    parts = np.concatenate([np.cos(fine), np.sin(fine), with_cos, with_sin, sums], axis=0)
    return np.pad(parts, ((0, -len(parts) % 8), (0, 0))).astype(np.float32)


def lag_table():
    real, imag = phase_table(np.arange(LAGS, dtype=np.int64) - LAGS // 2)
    rows = np.stack([real.reshape(GROUP, KB, LAGS), imag.reshape(GROUP, KB, LAGS)], axis=1)
    rows = rows.reshape(GROUP, ENT, LAGS).transpose(2, 0, 1)
    table = np.zeros((STEPS, LAG_ROWS, GROUP, STEPS, ENT), ml_dtypes.bfloat16)
    for step in range(STEPS):
        table[step, :LAGS, :, step, :] = rows
    return table.reshape(STEPS * LAG_ROWS, GROUP * STEPS * ENT)


def spread_rows():
    table = np.zeros((MIX * SB, NBLK * SB), ml_dtypes.bfloat16)
    for i in range(SB):
        for c in range(ENT):
            for b in range(NBLK):
                table[i * MIX + c * NBLK + b, b * SB + i] = 1
    return table


def pick_rows():
    half = ROUNDS // 2
    table = np.zeros((MIX * ROUNDS, SEEN * MIX), ml_dtypes.bfloat16)
    for h in range(2):
        for b in range(NBLK):
            for s in range(half):
                for c in range(ENT):
                    met = b + ROUNDS - (h * half + s + 1)
                    row = ((h * NBLK + b) * half + s) * ENT + c
                    table[row, met * MIX + c * NBLK + b] = 1
    return table


def spectra_kernel(records_ref, parts_ref, out_ref, x_ref, angle_ref, sems):
    copies = [
        pltpu.make_async_copy(
            records_ref.at[:, :, pl.ds(start, size)], x_ref.at[:, :, pl.ds(start, size)], sems.at[i]
        )
        for i, (start, size) in enumerate(PIECES)
    ]
    angles = pltpu.make_async_copy(parts_ref, angle_ref, sems.at[len(PIECES)])
    copies[0].start()
    angles.start()
    for copy in copies[1:]:
        copy.start()

    def samples(start, size):
        return x_ref[:, :, start : start + size].astype(jnp.float32).reshape(SB * DD, size)

    blocks = pl.cdiv(NT, BASE)
    raw = jnp.zeros((SB * DD, 2 * NB), jnp.float32)
    lanes = BASE // 2
    totals = jnp.zeros((SB * DD, lanes), jnp.float32)
    squares = jnp.zeros((SB * DD, lanes), jnp.float32)
    total = square = 0.0
    for i, (begin, length) in enumerate(PIECES):
        copies[i].wait()
        if i == 0:
            first_mean = jnp.sum(samples(begin, length), axis=1, keepdims=True) * (1.0 / length)
            angles.wait()
        for start in range(begin, begin + length, BASE):
            block, size = start // BASE, min(BASE, NT - start)
            with_cos = angle_ref[2 * BASE + block : 2 * BASE + block + 1, :]
            with_sin = angle_ref[2 * BASE + blocks + block : 2 * BASE + blocks + block + 1, :]
            table = with_cos * angle_ref[:size, :] + with_sin * angle_ref[BASE : BASE + size, :]
            x = samples(start, size) - first_mean
            if size == BASE:
                low, high = x[:, :lanes], x[:, lanes:]
                totals = totals + (low + high)
                squares = squares + (low * low + high * high)
            else:
                total = total + jnp.sum(x, axis=1, keepdims=True)
                square = square + jnp.sum(x * x, axis=1, keepdims=True)
            raw = raw + jnp.dot(
                x.astype(jnp.bfloat16), table.astype(jnp.bfloat16),
                preferred_element_type=jnp.float32,
            )
    total = total + jnp.sum(totals, axis=1, keepdims=True)
    square = square + jnp.sum(squares, axis=1, keepdims=True)
    rest = total * (1.0 / NT)
    raw = raw - rest * angle_ref[2 * BASE + 2 * blocks : 2 * BASE + 2 * blocks + 1, :]
    power = jnp.maximum(square * (1.0 / NT) - rest * rest, 0.0)
    raw = raw / jnp.sqrt(power + 1e-06)
    scale = jnp.sqrt(jnp.sum(raw * raw, axis=1, keepdims=True) * (1.0 / NB) + 1e-06)
    spectra = (raw / scale).astype(jnp.bfloat16)
    row = lax.broadcasted_iota(jnp.int32, (SB * DD, SB * DD), 0)
    column = lax.broadcasted_iota(jnp.int32, (SB * DD, SB * DD), 1)
    order = (row == column % SB * DD + column // SB).astype(jnp.float32).astype(jnp.bfloat16)
    by_entry = lax.dot_general(
        spectra, order, (((0,), (0,)), ((), ())), preferred_element_type=jnp.float32
    )
    for device in range(GROUP):
        out_ref[device] = by_entry[device * ENT : (device + 1) * ENT, :].astype(jnp.bfloat16)


def gather_days_kernel(r_ref, out_ref, wide_ref):
    turned = r_ref[...].astype(jnp.float32).T
    for e in range(DD):
        for b in range(NBLK):
            wide_ref[b * SB : (b + 1) * SB, e * WIDTH : (e + 1) * WIDTH] = (
                turned[e * SB : (e + 1) * SB, b * WIDTH : (b + 1) * WIDTH]
            )
    out_ref[...] = wide_ref[...].astype(jnp.bfloat16)


def cross_kernel(*refs):
    group_refs = refs[: BACK + 1]
    spread_ref, pick_ref, choice_ref, out_ref, met_ref, cross_ref, pair_ref = refs[BACK + 1 :]
    for step, group_ref in enumerate(group_refs):
        start = (BACK - step) * NBLK * SB
        met_ref[start : start + NBLK * SB, :] = group_ref[...]
    own = met_ref[BACK * NBLK * SB :, :]
    wide = own.astype(jnp.float32)
    lane = lax.broadcasted_iota(jnp.int32, wide.shape, 1)
    turned = jnp.where(
        lane % ENT < KB, pltpu.roll(wide, KDIM - KB, 1), -pltpu.roll(wide, KB, 1)
    ).astype(jnp.bfloat16)
    spread = spread_ref[...]
    row = lax.broadcasted_iota(jnp.int32, (MIX * SB, KDIM), 0)
    lane = lax.broadcasted_iota(jnp.int32, (MIX * SB, KDIM), 1)
    left = jnp.where(
        row % MIX < MIX // 2,
        jnp.dot(spread, own, preferred_element_type=jnp.float32),
        jnp.dot(spread, turned, preferred_element_type=jnp.float32),
    )
    left = jnp.where(row // NBLK % KB == lane % KB, left, 0.0).astype(jnp.bfloat16)
    cross_ref[...] = lax.dot_general(
        left, met_ref[...], (((1,), (1,)), ((), ())), preferred_element_type=jnp.float32
    )
    for i in range(SB):
        piece = cross_ref[i * MIX : (i + 1) * MIX, :]
        for met in range(SEEN):
            pair_ref[met * MIX : (met + 1) * MIX, i * SB : (i + 1) * SB] = (
                piece[:, met * SB : (met + 1) * SB]
            )
    picked = jnp.dot(
        pick_ref[...], pair_ref[...].astype(jnp.bfloat16), preferred_element_type=jnp.float32
    ).astype(jnp.bfloat16)
    chosen = jnp.dot(picked, choice_ref[...], preferred_element_type=jnp.float32)
    height = ROUNDS // 2 * ENT
    first = lax.broadcasted_iota(jnp.int32, (height, 2 * SHARE), 1) < SHARE
    for b in range(NBLK):
        for d in range(0, N_DAY, 2):
            low = chosen[b * height : (b + 1) * height, d * SHARE : (d + 2) * SHARE]
            high = chosen[
                (NBLK + b) * height : (NBLK + b + 1) * height, d * SHARE : (d + 2) * SHARE
            ]
            even = jnp.where(first, low, pltpu.roll(high, SHARE, 1))
            odd = jnp.where(first, pltpu.roll(low, SHARE, 1), high)
            out_ref[b * N_DAY + d] = even.astype(jnp.bfloat16)
            out_ref[b * N_DAY + d + 1] = odd.astype(jnp.bfloat16)


def lag_kernel(slot_ref, r_ref, lag_ref, out_ref):
    half = ROUNDS // 2
    lag = lag_ref[...]
    for first in range(0, half, STEPS):
        entries = r_ref[:, first * ENT : (first + STEPS) * ENT, :].reshape(
            GROUP * STEPS * ENT, 2 * SHARE
        )
        lagged = jnp.dot(lag, entries, preferred_element_type=jnp.float32)
        lagged = lagged * (1.0 / math.sqrt(NB * DD * N_DAY))
        for step in range(STEPS):
            turned = lagged[step * LAG_ROWS : (step + 1) * LAG_ROWS, :].T
            out_ref[slot_ref[first + step]] = turned[:SHARE, :LAGS]
            out_ref[slot_ref[half + first + step]] = turned[SHARE:, :LAGS]


def params():
    return pltpu.CompilerParams(vmem_limit_bytes=VMEM)


def vmem_specs(count):
    return [pl.BlockSpec(memory_space=pltpu.VMEM)] * count


def shards(records, offsets, pair_order):
    group_axes = ("zr", "xh", "day")
    parts = band_parts()
    spectra = pl.pallas_call(
        spectra_kernel,
        in_specs=[pl.BlockSpec(memory_space=pltpu.HBM)] * 2,
        out_specs=pl.BlockSpec(memory_space=pltpu.VMEM),
        out_shape=jax.ShapeDtypeStruct((GROUP, ENT, SB * DD), jnp.bfloat16),
        scratch_shapes=[
            pltpu.VMEM((SB, DD, NT), jnp.bfloat16),
            pltpu.VMEM(parts.shape, jnp.float32),
            pltpu.SemaphoreType.DMA((len(PIECES) + 1,)),
        ],
        compiler_params=pltpu.CompilerParams(vmem_limit_bytes=62 * 1024 * 1024),
        name="spectra",
    )(records, jnp.asarray(parts))

    by_bin = lax.all_to_all(spectra, group_axes, 0, 0, tiled=True).reshape(2 * NB, SB * DD)

    own = pl.pallas_call(
        gather_days_kernel,
        in_specs=vmem_specs(1),
        out_specs=pl.BlockSpec(memory_space=pltpu.VMEM),
        out_shape=jax.ShapeDtypeStruct((NBLK * SB, KDIM), jnp.bfloat16),
        scratch_shapes=[pltpu.VMEM((NBLK * SB, KDIM), jnp.float32)],
        compiler_params=params(),
        name="gather_days",
    )(by_bin)

    def moved(piece, steps):
        pairs = [(source, (source + steps) % GROUPS) for source in range(GROUPS)]
        return lax.ppermute(piece, "zq", pairs)

    met, far = [own], own
    for _ in range(BACK - 1):
        met.append(moved(met[-1], 1))
    for _ in range(2):
        far = moved(far, -(GROUPS - BACK) // 2)
    met.append(far)

    choice = (
        lax.broadcasted_iota(jnp.int32, (PAIRS, PAIRS), 0) == pair_order[None, :]
    ).astype(jnp.bfloat16)

    chosen = pl.pallas_call(
        cross_kernel,
        in_specs=vmem_specs(BACK + 4),
        out_specs=pl.BlockSpec(memory_space=pltpu.VMEM),
        out_shape=jax.ShapeDtypeStruct((GROUP, ROUNDS // 2 * ENT, 2 * SHARE), jnp.bfloat16),
        scratch_shapes=[
            pltpu.VMEM((SEEN * SB, KDIM), jnp.bfloat16),
            pltpu.VMEM((MIX * SB, SEEN * SB), jnp.float32),
            pltpu.VMEM((MIX * SEEN, PAIRS), jnp.float32),
        ],
        compiler_params=params(),
        name="cross",
    )(*met, jnp.asarray(spread_rows()), jnp.asarray(pick_rows()), choice)

    by_pair = lax.all_to_all(chosen, group_axes, 0, 0, tiled=True)

    steps = jnp.arange(ROUNDS, dtype=jnp.int32)
    slots = jnp.sum(
        jnp.where(offsets[None, :] == steps[:, None], steps[None, :], 0), axis=1
    ).astype(jnp.int32)

    lagged = pl.pallas_call(
        lag_kernel,
        in_specs=[pl.BlockSpec(memory_space=pltpu.SMEM)] + vmem_specs(2),
        out_specs=pl.BlockSpec(memory_space=pltpu.VMEM),
        out_shape=jax.ShapeDtypeStruct((ROUNDS, SHARE, LAGS), jnp.float32),
        compiler_params=params(),
        name="lags",
    )(slots, by_pair, jnp.asarray(lag_table()))
    return jnp.transpose(lagged, (0, 2, 1))


def solution(mesh):
    planes = mesh.shape["stn"] // N_HI
    devices = mesh.devices.reshape(planes // ZG, ZG, N_HI, mesh.shape["day"])
    fine = Mesh(devices, ("zq", "zr", "xh", "day"))
    stations = ("zq", "zr", "xh")
    in_specs = (P(stations, "day", None), P(), P())
    out_specs = P(None, None, stations + ("day",))
    return jax.shard_map(
        shards, mesh=fine, in_specs=in_specs, out_specs=out_specs, check_vma=False
    )
```

```python
import functools
import math

import jax
import jax.numpy as jnp
import ml_dtypes
import numpy as np
from jax import lax
from jax.experimental import pallas as pl
from jax.experimental.pallas import tpu as pltpu
from jax.sharding import Mesh
from jax.sharding import PartitionSpec as P

SB = 32
DD = 8
NT = 6000
NB = 128
K0 = 30
LAGS = 101
ROUNDS = 16
N_DAY = 16
N_HI = 2
PLANES = 16
ZG = 2
NBLK = ZG * N_HI
GROUP = NBLK * N_DAY
KB = NB // GROUP
ENT = 2 * KB
MIX = ENT * NBLK
GROUPS = PLANES // ZG
BACK = ROUNDS // NBLK
SEEN = ROUNDS + NBLK
WIDTH = N_DAY * ENT
KDIM = DD * WIDTH
PAIRS = SB * SB
SHARE = PAIRS // N_DAY
LAG_ROWS = 128
STEPS = 16 // ENT
BASE = 256
PIECE = 1536
PIECES = [(start, min(PIECE, NT - start)) for start in range(0, NT, PIECE)]
VMEM = 44 * 1024 * 1024

assert NB == GROUP * KB and ROUNDS == BACK * NBLK


def phase_table(columns):
    bins = np.arange(NB, dtype=np.int64) + K0
    turns = (bins[:, None] * columns[None, :]) % NT
    angle = 2.0 * math.pi / NT * turns.astype(np.float64)
    return np.cos(angle).astype(ml_dtypes.bfloat16), (-np.sin(angle)).astype(ml_dtypes.bfloat16)


def band_parts():
    bins = (np.arange(NB) + K0).reshape(GROUP, 1, KB)
    bins = np.broadcast_to(bins, (GROUP, 2, KB)).reshape(2 * NB).astype(np.int64)
    imag = np.broadcast_to(np.arange(2).reshape(1, 2, 1), (GROUP, 2, KB)).reshape(2 * NB)
    unit = 2.0 * math.pi / NT
    fine = unit * (np.arange(BASE)[:, None] * bins % NT)
    coarse = unit * (np.arange(0, NT, BASE)[:, None] * bins % NT)
    with_cos = np.where(imag, -np.sin(coarse), np.cos(coarse))
    with_sin = np.where(imag, -np.cos(coarse), -np.sin(coarse))
    real, imag = phase_table(np.arange(NT, dtype=np.int64))
    sums = np.stack([real.reshape(GROUP, KB, NT), imag.reshape(GROUP, KB, NT)], axis=1)
    sums = sums.astype(np.float64).sum(axis=3).reshape(1, 2 * NB)
    parts = np.concatenate([np.cos(fine), np.sin(fine), with_cos, with_sin, sums], axis=0)
    return np.pad(parts, ((0, -len(parts) % 8), (0, 0))).astype(np.float32)


def lag_table():
    real, imag = phase_table(np.arange(LAGS, dtype=np.int64) - LAGS // 2)
    rows = np.stack([real.reshape(GROUP, KB, LAGS), imag.reshape(GROUP, KB, LAGS)], axis=1)
    rows = rows.reshape(GROUP, ENT, LAGS).transpose(2, 0, 1)
    table = np.zeros((STEPS, LAG_ROWS, GROUP, STEPS, ENT), ml_dtypes.bfloat16)
    for step in range(STEPS):
        table[step, :LAGS, :, step, :] = rows
    return table.reshape(STEPS * LAG_ROWS, GROUP * STEPS * ENT)


def spread_rows():
    table = np.zeros((MIX * SB, NBLK * SB), ml_dtypes.bfloat16)
    for i in range(SB):
        for c in range(ENT):
            for b in range(NBLK):
                table[i * MIX + c * NBLK + b, b * SB + i] = 1
    return table


def pick_rows():
    half = ROUNDS // 2
    table = np.zeros((MIX * ROUNDS, SEEN * MIX), ml_dtypes.bfloat16)
    for h in range(2):
        for b in range(NBLK):
            for s in range(half):
                for c in range(ENT):
                    met = b + ROUNDS - (h * half + s + 1)
                    row = ((h * NBLK + b) * half + s) * ENT + c
                    table[row, met * MIX + c * NBLK + b] = 1
    return table


def spectra_kernel(records_ref, parts_ref, out_ref, x_ref, angle_ref, sems):
    copies = [
        pltpu.make_async_copy(
            records_ref.at[:, :, pl.ds(start, size)], x_ref.at[:, :, pl.ds(start, size)], sems.at[i]
        )
        for i, (start, size) in enumerate(PIECES)
    ]
    angles = pltpu.make_async_copy(parts_ref, angle_ref, sems.at[len(PIECES)])
    copies[0].start()
    angles.start()
    for copy in copies[1:]:
        copy.start()

    def samples(start, size):
        return x_ref[:, :, start : start + size].astype(jnp.float32).reshape(SB * DD, size)

    blocks = pl.cdiv(NT, BASE)
    raw = jnp.zeros((SB * DD, 2 * NB), jnp.float32)
    lanes = BASE // 2
    totals = jnp.zeros((SB * DD, lanes), jnp.float32)
    squares = jnp.zeros((SB * DD, lanes), jnp.float32)
    total = square = 0.0
    for i, (begin, length) in enumerate(PIECES):
        copies[i].wait()
        if i == 0:
            first_mean = jnp.sum(samples(begin, length), axis=1, keepdims=True) * (1.0 / length)
            angles.wait()
        for start in range(begin, begin + length, BASE):
            block, size = start // BASE, min(BASE, NT - start)
            with_cos = angle_ref[2 * BASE + block : 2 * BASE + block + 1, :]
            with_sin = angle_ref[2 * BASE + blocks + block : 2 * BASE + blocks + block + 1, :]
            table = with_cos * angle_ref[:size, :] + with_sin * angle_ref[BASE : BASE + size, :]
            x = samples(start, size) - first_mean
            if size == BASE:
                low, high = x[:, :lanes], x[:, lanes:]
                totals = totals + (low + high)
                squares = squares + (low * low + high * high)
            else:
                total = total + jnp.sum(x, axis=1, keepdims=True)
                square = square + jnp.sum(x * x, axis=1, keepdims=True)
            raw = raw + jnp.dot(
                x.astype(jnp.bfloat16), table.astype(jnp.bfloat16),
                preferred_element_type=jnp.float32,
            )
    total = total + jnp.sum(totals, axis=1, keepdims=True)
    square = square + jnp.sum(squares, axis=1, keepdims=True)
    rest = total * (1.0 / NT)
    raw = raw - rest * angle_ref[2 * BASE + 2 * blocks : 2 * BASE + 2 * blocks + 1, :]
    power = jnp.maximum(square * (1.0 / NT) - rest * rest, 0.0)
    raw = raw / jnp.sqrt(power + 1e-06)
    scale = jnp.sqrt(jnp.sum(raw * raw, axis=1, keepdims=True) * (1.0 / NB) + 1e-06)
    spectra = (raw / scale).astype(jnp.bfloat16)
    row = lax.broadcasted_iota(jnp.int32, (SB * DD, SB * DD), 0)
    column = lax.broadcasted_iota(jnp.int32, (SB * DD, SB * DD), 1)
    order = (row == column % SB * DD + column // SB).astype(jnp.float32).astype(jnp.bfloat16)
    by_entry = lax.dot_general(
        spectra, order, (((0,), (0,)), ((), ())), preferred_element_type=jnp.float32
    )
    for device in range(GROUP):
        out_ref[device] = by_entry[device * ENT : (device + 1) * ENT, :].astype(jnp.bfloat16)


def gather_days_kernel(r_ref, out_ref, wide_ref):
    turned = r_ref[...].astype(jnp.float32).T
    for e in range(DD):
        for b in range(NBLK):
            wide_ref[b * SB : (b + 1) * SB, e * WIDTH : (e + 1) * WIDTH] = (
                turned[e * SB : (e + 1) * SB, b * WIDTH : (b + 1) * WIDTH]
            )
    out_ref[...] = wide_ref[...].astype(jnp.bfloat16)


def cross_kernel(*refs):
    group_refs = refs[: BACK + 1]
    spread_ref, pick_ref, choice_ref, out_ref, met_ref, cross_ref, pair_ref = refs[BACK + 1 :]
    for step, group_ref in enumerate(group_refs):
        start = step * NBLK * SB
        met_ref[start : start + NBLK * SB, :] = group_ref[...]
    own = met_ref[BACK * NBLK * SB :, :]
    wide = own.astype(jnp.float32)
    lane = lax.broadcasted_iota(jnp.int32, wide.shape, 1)
    turned = jnp.where(
        lane % ENT < KB, pltpu.roll(wide, KDIM - KB, 1), -pltpu.roll(wide, KB, 1)
    ).astype(jnp.bfloat16)
    spread = spread_ref[...]
    row = lax.broadcasted_iota(jnp.int32, (MIX * SB, KDIM), 0)
    lane = lax.broadcasted_iota(jnp.int32, (MIX * SB, KDIM), 1)
    left = jnp.where(
        row % MIX < MIX // 2,
        jnp.dot(spread, own, preferred_element_type=jnp.float32),
        jnp.dot(spread, turned, preferred_element_type=jnp.float32),
    )
    left = jnp.where(row // NBLK % KB == lane % KB, left, 0.0).astype(jnp.bfloat16)
    cross_ref[...] = lax.dot_general(
        left, met_ref[...], (((1,), (1,)), ((), ())), preferred_element_type=jnp.float32
    )
    for i in range(SB):
        piece = cross_ref[i * MIX : (i + 1) * MIX, :]
        for met in range(SEEN):
            pair_ref[met * MIX : (met + 1) * MIX, i * SB : (i + 1) * SB] = (
                piece[:, met * SB : (met + 1) * SB]
            )
    picked = jnp.dot(
        pick_ref[...], pair_ref[...].astype(jnp.bfloat16), preferred_element_type=jnp.float32
    ).astype(jnp.bfloat16)
    chosen = jnp.dot(picked, choice_ref[...], preferred_element_type=jnp.float32)
    height = ROUNDS // 2 * ENT
    first = lax.broadcasted_iota(jnp.int32, (height, 2 * SHARE), 1) < SHARE
    for b in range(NBLK):
        for d in range(0, N_DAY, 2):
            low = chosen[b * height : (b + 1) * height, d * SHARE : (d + 2) * SHARE]
            high = chosen[
                (NBLK + b) * height : (NBLK + b + 1) * height, d * SHARE : (d + 2) * SHARE
            ]
            even = jnp.where(first, low, pltpu.roll(high, SHARE, 1))
            odd = jnp.where(first, pltpu.roll(low, SHARE, 1), high)
            out_ref[b * N_DAY + d] = even.astype(jnp.bfloat16)
            out_ref[b * N_DAY + d + 1] = odd.astype(jnp.bfloat16)


def lag_kernel(slot_ref, r_ref, lag_ref, out_ref, made_ref, sems):
    half = ROUNDS // 2
    copies = []
    lag = lag_ref[...]
    for first in range(0, half, STEPS):
        entries = r_ref[:, first * ENT : (first + STEPS) * ENT, :].reshape(
            GROUP * STEPS * ENT, 2 * SHARE
        )
        lagged = jnp.dot(lag, entries, preferred_element_type=jnp.float32)
        lagged = lagged * (1.0 / math.sqrt(NB * DD * N_DAY))
        for step in range(STEPS):
            turned = lagged[step * LAG_ROWS : (step + 1) * LAG_ROWS, :].T
            for round_step, part in (
                (first + step, turned[:SHARE, :LAGS]),
                (half + first + step, turned[SHARE:, :LAGS]),
            ):
                made_ref[round_step] = part
                copies.append(
                    pltpu.make_async_copy(
                        made_ref.at[round_step], out_ref.at[slot_ref[round_step]], sems.at[round_step]
                    )
                )
                copies[-1].start()
    for copy in copies:
        copy.wait()


def params():
    return pltpu.CompilerParams(vmem_limit_bytes=VMEM)


def vmem_specs(count):
    return [pl.BlockSpec(memory_space=pltpu.VMEM)] * count


def shards(records, offsets, pair_order):
    group_axes = ("zr", "xh", "day")
    parts = band_parts()
    spectra = pl.pallas_call(
        spectra_kernel,
        in_specs=[pl.BlockSpec(memory_space=pltpu.HBM)] * 2,
        out_specs=pl.BlockSpec(memory_space=pltpu.VMEM),
        out_shape=jax.ShapeDtypeStruct((GROUP, ENT, SB * DD), jnp.bfloat16),
        scratch_shapes=[
            pltpu.VMEM((SB, DD, NT), jnp.bfloat16),
            pltpu.VMEM(parts.shape, jnp.float32),
            pltpu.SemaphoreType.DMA((len(PIECES) + 1,)),
        ],
        compiler_params=pltpu.CompilerParams(vmem_limit_bytes=62 * 1024 * 1024),
        name="spectra",
    )(records, jnp.asarray(parts))

    by_bin = lax.all_to_all(spectra, group_axes, 0, 0, tiled=True).reshape(2 * NB, SB * DD)

    own = pl.pallas_call(
        gather_days_kernel,
        in_specs=vmem_specs(1),
        out_specs=pl.BlockSpec(memory_space=pltpu.VMEM),
        out_shape=jax.ShapeDtypeStruct((NBLK * SB, KDIM), jnp.bfloat16),
        scratch_shapes=[pltpu.VMEM((NBLK * SB, KDIM), jnp.float32)],
        compiler_params=params(),
        name="gather_days",
    )(by_bin)

    def moved(piece, steps):
        pairs = [(source, (source + steps) % GROUPS) for source in range(GROUPS)]
        return lax.ppermute(piece, "zq", pairs)

    half_way = moved(own, -(GROUPS - BACK) // 2)
    met = [own, moved(own, 1)]
    far = moved(half_way, -(GROUPS - BACK) // 2)
    for _ in range(BACK - 2):
        met.append(moved(met[-1], 1))
    met.append(far)

    choice = (
        lax.broadcasted_iota(jnp.int32, (PAIRS, PAIRS), 0) == pair_order[None, :]
    ).astype(jnp.bfloat16)

    chosen = pl.pallas_call(
        cross_kernel,
        in_specs=vmem_specs(BACK + 4),
        out_specs=pl.BlockSpec(memory_space=pltpu.VMEM),
        out_shape=jax.ShapeDtypeStruct((GROUP, ROUNDS // 2 * ENT, 2 * SHARE), jnp.bfloat16),
        scratch_shapes=[
            pltpu.VMEM((SEEN * SB, KDIM), jnp.bfloat16),
            pltpu.VMEM((MIX * SB, SEEN * SB), jnp.float32),
            pltpu.VMEM((MIX * SEEN, PAIRS), jnp.float32),
        ],
        compiler_params=params(),
        name="cross",
    )(*reversed(met), jnp.asarray(spread_rows()), jnp.asarray(pick_rows()), choice)

    by_pair = lax.all_to_all(chosen, group_axes, 0, 0, tiled=True)

    steps = jnp.arange(ROUNDS, dtype=jnp.int32)
    slots = jnp.sum(
        jnp.where(offsets[None, :] == steps[:, None], steps[None, :], 0), axis=1
    ).astype(jnp.int32)

    lagged = pl.pallas_call(
        lag_kernel,
        in_specs=[pl.BlockSpec(memory_space=pltpu.SMEM)] + vmem_specs(2),
        out_specs=pl.BlockSpec(memory_space=pltpu.HBM),
        out_shape=jax.ShapeDtypeStruct((ROUNDS, SHARE, LAGS), jnp.float32),
        scratch_shapes=[
            pltpu.VMEM((ROUNDS, SHARE, LAGS), jnp.float32),
            pltpu.SemaphoreType.DMA((ROUNDS,)),
        ],
        compiler_params=params(),
        name="lags",
    )(slots, by_pair, jnp.asarray(lag_table()))
    return jnp.transpose(lagged, (0, 2, 1))


def solution(mesh):
    planes = mesh.shape["stn"] // N_HI
    devices = mesh.devices.reshape(planes // ZG, ZG, N_HI, mesh.shape["day"])
    fine = Mesh(devices, ("zq", "zr", "xh", "day"))
    stations = ("zq", "zr", "xh")
    in_specs = (P(stations, "day", None), P(), P())
    out_specs = P(None, None, stations + ("day",))
    return jax.shard_map(
        shards, mesh=fine, in_specs=in_specs, out_specs=out_specs, check_vma=False
    )
```

```python
import functools
import math

import jax
import jax.numpy as jnp
import ml_dtypes
import numpy as np
from jax import lax
from jax.experimental import pallas as pl
from jax.experimental.pallas import tpu as pltpu
from jax.sharding import Mesh
from jax.sharding import PartitionSpec as P

SB = 32
DD = 8
NT = 6000
NB = 128
K0 = 30
LAGS = 101
ROUNDS = 16
N_DAY = 16
N_HI = 2
PLANES = 16
ZG = 2
NBLK = ZG * N_HI
GROUP = NBLK * N_DAY
KB = NB // GROUP
ENT = 2 * KB
MIX = ENT * NBLK
GROUPS = PLANES // ZG
BACK = ROUNDS // NBLK
SEEN = ROUNDS + NBLK
WIDTH = N_DAY * ENT
KDIM = DD * WIDTH
PAIRS = SB * SB
SHARE = PAIRS // N_DAY
LAG_ROWS = 128
STEPS = 16 // ENT
BASE = 256
PIECE = 1536
PIECES = [(start, min(PIECE, NT - start)) for start in range(0, NT, PIECE)]
VMEM = 44 * 1024 * 1024

assert NB == GROUP * KB and ROUNDS == BACK * NBLK


def phase_table(columns):
    bins = np.arange(NB, dtype=np.int64) + K0
    turns = (bins[:, None] * columns[None, :]) % NT
    angle = 2.0 * math.pi / NT * turns.astype(np.float64)
    return np.cos(angle).astype(ml_dtypes.bfloat16), (-np.sin(angle)).astype(ml_dtypes.bfloat16)


def band_parts():
    bins = (np.arange(NB) + K0).reshape(GROUP, 1, KB)
    bins = np.broadcast_to(bins, (GROUP, 2, KB)).reshape(2 * NB).astype(np.int64)
    imag = np.broadcast_to(np.arange(2).reshape(1, 2, 1), (GROUP, 2, KB)).reshape(2 * NB)
    unit = 2.0 * math.pi / NT
    fine = unit * (np.arange(BASE)[:, None] * bins % NT)
    coarse = unit * (np.arange(0, NT, BASE)[:, None] * bins % NT)
    with_cos = np.where(imag, -np.sin(coarse), np.cos(coarse))
    with_sin = np.where(imag, -np.cos(coarse), -np.sin(coarse))
    real, imag = phase_table(np.arange(NT, dtype=np.int64))
    sums = np.stack([real.reshape(GROUP, KB, NT), imag.reshape(GROUP, KB, NT)], axis=1)
    sums = sums.astype(np.float64).sum(axis=3).reshape(1, 2 * NB)
    parts = np.concatenate([np.cos(fine), np.sin(fine), with_cos, with_sin, sums], axis=0)
    return np.pad(parts, ((0, -len(parts) % 8), (0, 0))).astype(np.float32)


def lag_table():
    real, imag = phase_table(np.arange(LAGS, dtype=np.int64) - LAGS // 2)
    rows = np.stack([real.reshape(GROUP, KB, LAGS), imag.reshape(GROUP, KB, LAGS)], axis=1)
    rows = rows.reshape(GROUP, ENT, LAGS).transpose(2, 0, 1)
    table = np.zeros((STEPS, LAG_ROWS, GROUP, STEPS, ENT), ml_dtypes.bfloat16)
    for step in range(STEPS):
        table[step, :LAGS, :, step, :] = rows
    return table.reshape(STEPS * LAG_ROWS, GROUP * STEPS * ENT)


def spread_rows():
    table = np.zeros((MIX * SB, NBLK * SB), ml_dtypes.bfloat16)
    for i in range(SB):
        for c in range(ENT):
            for b in range(NBLK):
                table[i * MIX + c * NBLK + b, b * SB + i] = 1
    return table


def pick_rows():
    half = ROUNDS // 2
    table = np.zeros((MIX * ROUNDS, SEEN * MIX), ml_dtypes.bfloat16)
    for h in range(2):
        for b in range(NBLK):
            for s in range(half):
                for c in range(ENT):
                    met = b + ROUNDS - (h * half + s + 1)
                    row = ((h * NBLK + b) * half + s) * ENT + c
                    table[row, met * MIX + c * NBLK + b] = 1
    return table


def spectra_kernel(records_ref, parts_ref, out_ref, x_ref, angle_ref, sems):
    copies = [
        pltpu.make_async_copy(
            records_ref.at[:, :, pl.ds(start, size)], x_ref.at[:, :, pl.ds(start, size)], sems.at[i]
        )
        for i, (start, size) in enumerate(PIECES)
    ]
    angles = pltpu.make_async_copy(parts_ref, angle_ref, sems.at[len(PIECES)])
    copies[0].start()
    angles.start()
    for copy in copies[1:]:
        copy.start()

    def samples(start, size):
        return x_ref[:, :, start : start + size].astype(jnp.float32).reshape(SB * DD, size)

    blocks = pl.cdiv(NT, BASE)
    raw = jnp.zeros((SB * DD, 2 * NB), jnp.float32)
    lanes = BASE // 2
    totals = jnp.zeros((SB * DD, lanes), jnp.float32)
    squares = jnp.zeros((SB * DD, lanes), jnp.float32)
    total = square = 0.0
    for i, (begin, length) in enumerate(PIECES):
        copies[i].wait()
        if i == 0:
            first_mean = jnp.sum(samples(begin, length), axis=1, keepdims=True) * (1.0 / length)
            angles.wait()
        for start in range(begin, begin + length, BASE):
            block, size = start // BASE, min(BASE, NT - start)
            with_cos = angle_ref[2 * BASE + block : 2 * BASE + block + 1, :]
            with_sin = angle_ref[2 * BASE + blocks + block : 2 * BASE + blocks + block + 1, :]
            table = with_cos * angle_ref[:size, :] + with_sin * angle_ref[BASE : BASE + size, :]
            x = samples(start, size) - first_mean
            if size == BASE:
                low, high = x[:, :lanes], x[:, lanes:]
                totals = totals + (low + high)
                squares = squares + (low * low + high * high)
            else:
                total = total + jnp.sum(x, axis=1, keepdims=True)
                square = square + jnp.sum(x * x, axis=1, keepdims=True)
            raw = raw + jnp.dot(
                x.astype(jnp.bfloat16), table.astype(jnp.bfloat16),
                preferred_element_type=jnp.float32,
            )
    total = total + jnp.sum(totals, axis=1, keepdims=True)
    square = square + jnp.sum(squares, axis=1, keepdims=True)
    rest = total * (1.0 / NT)
    raw = raw - rest * angle_ref[2 * BASE + 2 * blocks : 2 * BASE + 2 * blocks + 1, :]
    power = jnp.maximum(square * (1.0 / NT) - rest * rest, 0.0)
    raw = raw / jnp.sqrt(power + 1e-06)
    scale = jnp.sqrt(jnp.sum(raw * raw, axis=1, keepdims=True) * (1.0 / NB) + 1e-06)
    spectra = (raw / scale).astype(jnp.bfloat16)
    row = lax.broadcasted_iota(jnp.int32, (SB * DD, SB * DD), 0)
    column = lax.broadcasted_iota(jnp.int32, (SB * DD, SB * DD), 1)
    order = (row == column % SB * DD + column // SB).astype(jnp.float32).astype(jnp.bfloat16)
    by_entry = lax.dot_general(
        spectra, order, (((0,), (0,)), ((), ())), preferred_element_type=jnp.float32
    )
    for device in range(GROUP):
        out_ref[device] = by_entry[device * ENT : (device + 1) * ENT, :].astype(jnp.bfloat16)


def gather_days_kernel(r_ref, out_ref, wide_ref):
    turned = r_ref[...].astype(jnp.float32).T
    for e in range(DD):
        for b in range(NBLK):
            wide_ref[b * SB : (b + 1) * SB, e * WIDTH : (e + 1) * WIDTH] = (
                turned[e * SB : (e + 1) * SB, b * WIDTH : (b + 1) * WIDTH]
            )
    out_ref[...] = wide_ref[...].astype(jnp.bfloat16)


def cross_kernel(*refs):
    group_refs = refs[: BACK + 1]
    spread_ref, pick_ref, choice_ref, out_ref, met_ref, cross_ref, pair_ref = refs[BACK + 1 :]
    for step, group_ref in enumerate(group_refs):
        start = step * NBLK * SB
        met_ref[start : start + NBLK * SB, :] = group_ref[...]
    own = met_ref[BACK * NBLK * SB :, :]
    wide = own.astype(jnp.float32)
    lane = lax.broadcasted_iota(jnp.int32, wide.shape, 1)
    turned = jnp.where(
        lane % ENT < KB, pltpu.roll(wide, KDIM - KB, 1), -pltpu.roll(wide, KB, 1)
    ).astype(jnp.bfloat16)
    spread = spread_ref[...]
    row = lax.broadcasted_iota(jnp.int32, (MIX * SB, KDIM), 0)
    lane = lax.broadcasted_iota(jnp.int32, (MIX * SB, KDIM), 1)
    left = jnp.where(
        row % MIX < MIX // 2,
        jnp.dot(spread, own, preferred_element_type=jnp.float32),
        jnp.dot(spread, turned, preferred_element_type=jnp.float32),
    )
    left = jnp.where(row // NBLK % KB == lane % KB, left, 0.0).astype(jnp.bfloat16)
    cross_ref[...] = lax.dot_general(
        left, met_ref[...], (((1,), (1,)), ((), ())), preferred_element_type=jnp.float32
    )
    for i in range(SB):
        piece = cross_ref[i * MIX : (i + 1) * MIX, :]
        for met in range(SEEN):
            pair_ref[met * MIX : (met + 1) * MIX, i * SB : (i + 1) * SB] = (
                piece[:, met * SB : (met + 1) * SB]
            )
    picked = jnp.dot(
        pick_ref[...], pair_ref[...].astype(jnp.bfloat16), preferred_element_type=jnp.float32
    ).astype(jnp.bfloat16)
    chosen = jnp.dot(picked, choice_ref[...], preferred_element_type=jnp.float32)
    height = ROUNDS // 2 * ENT
    first = lax.broadcasted_iota(jnp.int32, (height, 2 * SHARE), 1) < SHARE
    for b in range(NBLK):
        for d in range(0, N_DAY, 2):
            low = chosen[b * height : (b + 1) * height, d * SHARE : (d + 2) * SHARE]
            high = chosen[
                (NBLK + b) * height : (NBLK + b + 1) * height, d * SHARE : (d + 2) * SHARE
            ]
            even = jnp.where(first, low, pltpu.roll(high, SHARE, 1))
            odd = jnp.where(first, pltpu.roll(low, SHARE, 1), high)
            out_ref[b * N_DAY + d] = even.astype(jnp.bfloat16)
            out_ref[b * N_DAY + d + 1] = odd.astype(jnp.bfloat16)


def lag_kernel(slot_ref, r_ref, lag_ref, out_ref, made_ref, sems):
    half = ROUNDS // 2
    copies = []
    lag = lag_ref[...]
    for first in range(0, half, STEPS):
        entries = r_ref[:, first * ENT : (first + STEPS) * ENT, :].reshape(
            GROUP * STEPS * ENT, 2 * SHARE
        )
        lagged = jnp.dot(lag, entries, preferred_element_type=jnp.float32)
        lagged = lagged * (1.0 / math.sqrt(NB * DD * N_DAY))
        for step in range(STEPS):
            turned = lagged[step * LAG_ROWS : (step + 1) * LAG_ROWS, :].T
            for round_step, part in (
                (first + step, turned[:SHARE, :LAGS]),
                (half + first + step, turned[SHARE:, :LAGS]),
            ):
                made_ref[round_step] = part
                copies.append(
                    pltpu.make_async_copy(
                        made_ref.at[round_step], out_ref.at[slot_ref[round_step]], sems.at[round_step]
                    )
                )
                copies[-1].start()
    for copy in copies:
        copy.wait()


def params():
    return pltpu.CompilerParams(vmem_limit_bytes=VMEM)


def vmem_specs(count):
    return [pl.BlockSpec(memory_space=pltpu.VMEM)] * count


def shards(records, offsets, pair_order):
    group_axes = ("zr", "xh", "day")
    parts = band_parts()
    spectra = pl.pallas_call(
        spectra_kernel,
        in_specs=[pl.BlockSpec(memory_space=pltpu.HBM)] * 2,
        out_specs=pl.BlockSpec(memory_space=pltpu.VMEM),
        out_shape=jax.ShapeDtypeStruct((GROUP, ENT, SB * DD), jnp.bfloat16),
        scratch_shapes=[
            pltpu.VMEM((SB, DD, NT), jnp.bfloat16),
            pltpu.VMEM(parts.shape, jnp.float32),
            pltpu.SemaphoreType.DMA((len(PIECES) + 1,)),
        ],
        compiler_params=pltpu.CompilerParams(vmem_limit_bytes=62 * 1024 * 1024),
        name="spectra",
    )(records, jnp.asarray(parts))

    by_bin = lax.all_to_all(spectra, group_axes, 0, 0, tiled=True).reshape(2 * NB, SB * DD)

    own = pl.pallas_call(
        gather_days_kernel,
        in_specs=vmem_specs(1),
        out_specs=pl.BlockSpec(memory_space=pltpu.VMEM),
        out_shape=jax.ShapeDtypeStruct((NBLK * SB, KDIM), jnp.bfloat16),
        scratch_shapes=[pltpu.VMEM((NBLK * SB, KDIM), jnp.float32)],
        compiler_params=params(),
        name="gather_days",
    )(by_bin)

    def moved(piece, steps):
        pairs = [(source, (source + steps) % GROUPS) for source in range(GROUPS)]
        return lax.ppermute(piece, "zq", pairs)

    met = [own]
    for _ in range(BACK - 1):
        met.append(moved(met[-1], 1))
    met.append(moved(own, BACK))

    choice = (
        lax.broadcasted_iota(jnp.int32, (PAIRS, PAIRS), 0) == pair_order[None, :]
    ).astype(jnp.bfloat16)

    chosen = pl.pallas_call(
        cross_kernel,
        in_specs=vmem_specs(BACK + 4),
        out_specs=pl.BlockSpec(memory_space=pltpu.VMEM),
        out_shape=jax.ShapeDtypeStruct((GROUP, ROUNDS // 2 * ENT, 2 * SHARE), jnp.bfloat16),
        scratch_shapes=[
            pltpu.VMEM((SEEN * SB, KDIM), jnp.bfloat16),
            pltpu.VMEM((MIX * SB, SEEN * SB), jnp.float32),
            pltpu.VMEM((MIX * SEEN, PAIRS), jnp.float32),
        ],
        compiler_params=params(),
        name="cross",
    )(*reversed(met), jnp.asarray(spread_rows()), jnp.asarray(pick_rows()), choice)

    by_pair = lax.all_to_all(chosen, group_axes, 0, 0, tiled=True)

    steps = jnp.arange(ROUNDS, dtype=jnp.int32)
    slots = jnp.sum(
        jnp.where(offsets[None, :] == steps[:, None], steps[None, :], 0), axis=1
    ).astype(jnp.int32)

    lagged = pl.pallas_call(
        lag_kernel,
        in_specs=[pl.BlockSpec(memory_space=pltpu.SMEM)] + vmem_specs(2),
        out_specs=pl.BlockSpec(memory_space=pltpu.HBM),
        out_shape=jax.ShapeDtypeStruct((ROUNDS, SHARE, LAGS), jnp.float32),
        scratch_shapes=[
            pltpu.VMEM((ROUNDS, SHARE, LAGS), jnp.float32),
            pltpu.SemaphoreType.DMA((ROUNDS,)),
        ],
        compiler_params=params(),
        name="lags",
    )(slots, by_pair, jnp.asarray(lag_table()))
    return jnp.transpose(lagged, (0, 2, 1))


def solution(mesh):
    planes = mesh.shape["stn"] // N_HI
    devices = mesh.devices.reshape(planes // ZG, ZG, N_HI, mesh.shape["day"])
    fine = Mesh(devices, ("zq", "zr", "xh", "day"))
    stations = ("zq", "zr", "xh")
    in_specs = (P(stations, "day", None), P(), P())
    out_specs = P(None, None, stations + ("day",))
    return jax.shard_map(
        shards, mesh=fine, in_specs=in_specs, out_specs=out_specs, check_vma=False
    )
```
